128 devices in a mesh: grid: 32 (over x, z, core), rep: 4 (over y).
Axes of the slice: x: 4, y: 4, z: 4, core: 2. Of those that a mesh axis runs over, the one named last changes fastest.
Arguments:
- density: bfloat16 [4096, 4096], P('grid', 'rep'), may hold values from -4.5 to 4.5
- pattern: int32 [32, 32], replicated, may hold values from 0 to 1, as said below
Outputs:
- sign_matrix: float32 [4096, 4096], P('grid', 'rep')
The draws below stay inside these ranges and needn't reach their ends.
Inputs may be any that keep to these rules, and one draw needn't show every extreme that they name: `pattern`: Symmetric, with ones on the diagonal and beside it.
All inputs are finite; a program needn't handle non-finite values.
Results may differ from the reference program's by a relative error of at most 0.0035.
Values may be sent and summed in bfloat16 or wider, within the bound.
A program may use at most 64 MiB of HBM per device.

```python
import jax
import jax.numpy as jnp
from jax import lax

BLOCK = 128
STEPS = 2
NB = 32
ORDER = 4096


def draw_pattern(key, part):
    key = jax.random.fold_in(key, 11)
    first_key, second_key = jax.random.split(key, 2)
    weights = jax.random.randint(first_key, (NB,), 1, 5)
    levels = jax.random.randint(second_key, (NB, NB), 0, 1000)
    symmetric = jnp.triu(levels) + jnp.triu(levels, 1).T
    block_index = jnp.arange(NB)
    adjacent = jnp.abs(block_index[:, None] - block_index[None, :]) <= 1
    occupied = (symmetric < 100 * weights[:, None] * weights[None, :]) | adjacent
    return occupied.astype(jnp.int32)


def draw_density(key, part):
    key = jax.random.fold_in(key, 23)
    first_key = jax.random.fold_in(key, 0)
    entries = jnp.clip(jax.random.normal(first_key, (ORDER, ORDER), jnp.float32), -4.5, 4.5)
    return entries.astype(jnp.bfloat16)


def setup_inputs(seed: int = 0) -> dict:
    arg_keys = jax.random.split(jax.random.key(seed), 3)
    density = draw_density(jax.random.fold_in(arg_keys[2], 71), 0)
    pattern = draw_pattern(jax.random.fold_in(arg_keys[2], 71), 0)
    return {"density": density, "pattern": pattern}


def expand_pattern(pattern):
    return jnp.repeat(jnp.repeat(pattern, BLOCK, axis=0), BLOCK, axis=1) > 0


def outer_product(first, second):
    return jnp.dot(first.astype(jnp.float32), second.astype(jnp.float32).T, precision=lax.Precision.HIGHEST)


def reference(density, pattern):
    keep_mask = expand_pattern(pattern)
    state = jnp.where(keep_mask, density, jnp.zeros_like(density))
    for iteration in range(STEPS):
        square = jnp.where(keep_mask, outer_product(state, state) / ORDER, jnp.float32(0.0)).astype(jnp.bfloat16)
        cubic = outer_product(state, square)
        updated = jnp.where(keep_mask, 1.5 * state.astype(jnp.float32) - 0.5 * cubic, jnp.float32(0.0))
        if iteration + 1 < STEPS:
            state = updated.astype(jnp.bfloat16)
        else:
            state = updated
    return state
```

```python
import jax
import jax.numpy as jnp
from jax import lax
from jax.experimental import pallas as pl
from jax.experimental.pallas import tpu as pltpu
from jax.sharding import PartitionSpec as P

BLOCK = 128
STEPS = 2
ORDER = 4096
MESH = pl.DeviceIdType.MESH
RING = 4
PAIR = 2 * BLOCK
FAR_FIRST = (2, 1, 3)
NEAR_FIRST = (1, 3, 2)

GATHER_I = 0
GATHER_J = 3
SIBLING = 6
REDUCE_Q = 10
GATHER_Q = 22
REDUCE_C = 34
RELAY = 46
TURNED = 49
HAND_OVER = 52
SLOTS = 56


def nt_dot(left, right):
    return lax.dot_general(left, right, (((1,), (1,)), ((), ())), preferred_element_type=jnp.float32)


def block_of(outer, z, core):
    return outer * 8 + z * 2 + core


def kernel(density, pattern, out, rows_i, rows_j, send_q, got_q, own_q, square, send_c, got_c, own_c,
           unit, relay, turned, final, got_final, send_sem, recv_sem):
    grid_pos = lax.axis_index("grid")
    y = lax.axis_index("rep")
    x = grid_pos // 8
    z = (grid_pos // 2) % 4
    core = grid_pos % 2

    def device(step, p, q, z_at, core_at):
        x_at, y_at = (p, q) if step == 0 else (q, p)
        return ((x_at * 4 + z_at) * 2 + core_at, y_at)

    def copy(src, dst, step, slot, target):
        at = step * SLOTS + slot
        return pltpu.make_async_remote_copy(
            src_ref=src, dst_ref=dst, send_sem=send_sem.at[at], recv_sem=recv_sem.at[at],
            device_id=target, device_id_type=MESH,
        )

    def rows(start, size):
        return pl.ds(pl.multiple_of(start, size), size)

    def turn(a, d):
        return (a + d) % RING

    barrier = pltpu.get_barrier_semaphore()
    partners = [device(0, x, y, z, 1 - core)]
    for d in (1, 2, 3):
        partners += [device(0, turn(x, d), y, z, core), device(0, x, turn(y, d), z, core),
                     device(0, x, y, turn(z, d), core)]
    for partner in partners:
        pl.semaphore_signal(barrier, inc=1, device_id=partner, device_id_type=MESH)

    def keep(row_block, col_block):
        return pattern[row_block, col_block].astype(jnp.float32)

    mine = rows(x * PAIR + core * BLOCK, BLOCK)
    for b in range(8):
        cols = pl.ds(b * BLOCK, BLOCK)
        masked = density[:, cols].astype(jnp.float32) * keep(block_of(x, z, core), y * 8 + b)
        rows_j[0, mine, cols] = masked.astype(jnp.bfloat16)
    pl.semaphore_wait(barrier, len(partners))

    sends = []

    def start(c):
        c.start()
        sends.append(c)

    for step in range(STEPS):
        p, q = (x, y) if step == 0 else (y, x)
        here = device(step, p, q, z, core)
        sibling = device(step, p, q, z, 1 - core)
        own = rows(p * PAIR + core * BLOCK, BLOCK)
        own_src = rows_j.at[step, own]

        def arrival(dst, slot, step=step, here=here):
            return copy(dst, dst, step, slot, here)

        for d in NEAR_FIRST:
            start(copy(own_src, rows_j.at[step, own], step, GATHER_J + d - 1, device(step, turn(p, d), q, z, core)))
            start(copy(own_src, rows_i.at[step, rows(z * BLOCK, BLOCK)], step, GATHER_I + d - 1,
                       device(step, p, q, turn(z, d), core)))
        if step == 0:
            start(copy(own_src, own_src, step, SIBLING, sibling))
        rows_i[step, rows(z * BLOCK, BLOCK), :] = rows_j[step, own, :]
        if step == 0:
            arrival(rows_j.at[step, rows(p * PAIR + (1 - core) * BLOCK, BLOCK)], SIBLING).wait_recv()
            for b in range(4):
                unit[0, :, pl.ds(b * BLOCK, BLOCK)] = rows_j[0, rows(p * PAIR, PAIR), rows((2 * b + core) * BLOCK, BLOCK)]
        lag = turn(p - q, RING)

        @pl.when(lag != 0)
        def _(step=step, p=p, q=q, lag=lag):
            copy(unit.at[step], relay.at[step, lag - 1], step, RELAY + lag - 1, device(step, p, p, z, core)).start()

        for d in NEAR_FIRST:
            there = rows_j.at[step, rows(turn(p, RING - d) * PAIR + core * BLOCK, BLOCK)]
            arrival(there, GATHER_J + d - 1).wait_recv()
            start(copy(there, there, step, SIBLING + d, sibling))
        for d in NEAR_FIRST:
            arrival(rows_i.at[step, rows(turn(z, RING - d) * BLOCK, BLOCK)], GATHER_I + d - 1).wait_recv()
        for d in NEAR_FIRST:
            arrival(rows_j.at[step, rows(turn(p, RING - d) * PAIR + (1 - core) * BLOCK, BLOCK)], SIBLING + d).wait_recv()

        for half in range(2):
            lines = pl.ds(half * PAIR, PAIR)
            left = rows_i[step, lines, :]
            for d in FAR_FIRST:
                send_q[step, d - 1, lines, :] = nt_dot(left, rows_j[step, rows(turn(q, d) * PAIR, PAIR), :]).astype(jnp.bfloat16)
            for chunk in (2 * half, 2 * half + 1):
                part = pl.ds(chunk * BLOCK, BLOCK)
                for d in FAR_FIRST:
                    start(copy(send_q.at[step, d - 1, part], got_q.at[step, d - 1, part], step,
                               REDUCE_Q + 3 * chunk + d - 1, device(step, p, turn(q, d), z, core)))
            own_q[lines, :] = nt_dot(left, rows_j[step, rows(q * PAIR, PAIR), :])

        @pl.when(lag == 0)
        def _(step=step, p=p, q=q, here=here):
            for d in (1, 2, 3):
                copy(relay.at[step, d - 1], relay.at[step, d - 1], step, RELAY + d - 1, here).wait_recv()
                copy(relay.at[step, d - 1], turned.at[step], step, TURNED + d - 1, device(step, turn(p, RING - d), q, z, core)).start()
            turned[step] = unit[step]

        def add_square(chunk, step=step, p=p, q=q):
            part = pl.ds(chunk * BLOCK, BLOCK)
            total = own_q[part, :]
            for d in FAR_FIRST:
                arrival(got_q.at[step, d - 1, part], REDUCE_Q + 3 * chunk + d - 1).wait_recv()
                total += got_q[step, d - 1, part, :].astype(jnp.float32)
            for b in range(2):
                scale = keep(block_of(p, chunk, core), block_of(q, z, b)) * (1.0 / ORDER)
                square[step, part, rows(z * PAIR + b * BLOCK, BLOCK)] = (
                    total[:, b * BLOCK:(b + 1) * BLOCK] * scale).astype(jnp.bfloat16)
            block = square.at[step, part, rows(z * PAIR, PAIR)]
            for d in NEAR_FIRST:
                start(copy(block, block, step, GATHER_Q + 3 * chunk + d - 1, device(step, p, q, turn(z, d), core)))

        def cubic_terms(chunk, step=step, p=p, q=q):
            part = pl.ds(chunk * BLOCK, BLOCK)
            for d in NEAR_FIRST:
                arrival(square.at[step, part, rows(turn(z, RING - d) * PAIR, PAIR)], GATHER_Q + 3 * chunk + d - 1).wait_recv()
            right = square[step, part, :]
            for d in FAR_FIRST:
                send_c[step, d - 1, chunk] = nt_dot(rows_j[step, rows(turn(q, d) * PAIR, PAIR), :], right).astype(jnp.bfloat16)
                start(copy(send_c.at[step, d - 1, chunk], got_c.at[step, d - 1, chunk], step,
                           REDUCE_C + 3 * chunk + d - 1, device(step, p, turn(q, d), z, core)))
            own_c[chunk] = nt_dot(rows_j[step, rows(q * PAIR, PAIR), :], right)

        def add_cubic(chunk, step=step, p=p, q=q, sibling=sibling):
            total = own_c[chunk]
            for d in FAR_FIRST:
                arrival(got_c.at[step, d - 1, chunk], REDUCE_C + 3 * chunk + d - 1).wait_recv()
                total += got_c[step, d - 1, chunk].astype(jnp.float32)
            updated = 1.5 * turned[step, :, pl.ds(chunk * BLOCK, BLOCK)].astype(jnp.float32) - 0.5 * total
            halves = [updated[b * BLOCK:(b + 1) * BLOCK] * keep(block_of(q, z, b), block_of(p, chunk, core)) for b in range(2)]
            if step + 1 < STEPS:
                cols = pl.ds(chunk * BLOCK, BLOCK)
                for b in range(2):
                    unit[step + 1, pl.ds(b * BLOCK, BLOCK), cols] = halves[b].astype(jnp.bfloat16)
                place = rows_j.at[step + 1, rows(q * PAIR, PAIR), rows((2 * chunk + core) * BLOCK, BLOCK)]
                place[...] = unit[step + 1, :, cols]
                start(copy(place, place, step, HAND_OVER + chunk, sibling))
            else:
                for b in range(2):
                    final[chunk, pl.ds(b * BLOCK, BLOCK), :] = halves[b]
                out[:, rows((2 * chunk + core) * BLOCK, BLOCK)] = final[chunk, rows(core * BLOCK, BLOCK), :]
                start(copy(final.at[chunk, rows((1 - core) * BLOCK, BLOCK)], got_final.at[chunk], step,
                           HAND_OVER + chunk, sibling))

        add_square(0)
        add_square(1)
        add_square(2)
        cubic_terms(0)
        add_square(3)
        cubic_terms(1)
        cubic_terms(2)

        @pl.when(lag != 0)
        def _(step=step, here=here, lag=lag):
            copy(turned.at[step], turned.at[step], step, TURNED + RING - lag - 1, here).wait_recv()

        add_cubic(0)
        cubic_terms(3)
        add_cubic(1)
        add_cubic(2)
        add_cubic(3)
        for chunk in range(4):
            cols = rows((2 * chunk + 1 - core) * BLOCK, BLOCK)
            if step + 1 < STEPS:
                arrival(rows_j.at[step + 1, rows(q * PAIR, PAIR), cols], HAND_OVER + chunk).wait_recv()
            else:
                arrival(got_final.at[chunk], HAND_OVER + chunk).wait_recv()
                out[:, cols] = got_final[chunk]

    for c in sends:
        c.wait_send()
    for step in range(STEPS):
        p, q = (x, y) if step == 0 else (y, x)
        lag = turn(p - q, RING)

        @pl.when(lag != 0)
        def _(step=step, p=p, q=q, lag=lag):
            copy(unit.at[step], relay.at[step, lag - 1], step, RELAY + lag - 1, device(step, p, p, z, core)).wait_send()

        @pl.when(lag == 0)
        def _(step=step, p=p, q=q):
            for d in (1, 2, 3):
                copy(relay.at[step, d - 1], turned.at[step], step, TURNED + d - 1, device(step, turn(p, RING - d), q, z, core)).wait_send()


def per_device(density, pattern):
    bf16, f32 = jnp.bfloat16, jnp.float32
    quarter = ORDER // RING
    return pl.pallas_call(
        kernel,
        out_shape=jax.ShapeDtypeStruct(density.shape, f32),
        in_specs=[pl.BlockSpec(memory_space=pltpu.VMEM), pl.BlockSpec(memory_space=pltpu.SMEM)],
        out_specs=pl.BlockSpec(memory_space=pltpu.VMEM),
        scratch_shapes=[
            pltpu.VMEM((STEPS, 4 * BLOCK, quarter), bf16),
            pltpu.VMEM((STEPS, 8 * BLOCK, quarter), bf16),
            pltpu.VMEM((STEPS, 3, 4 * BLOCK, PAIR), bf16),
            pltpu.VMEM((STEPS, 3, 4 * BLOCK, PAIR), bf16),
            pltpu.VMEM((4 * BLOCK, PAIR), f32),
            pltpu.VMEM((STEPS, 4 * BLOCK, quarter), bf16),
            pltpu.VMEM((STEPS, 3, 4, PAIR, BLOCK), bf16),
            pltpu.VMEM((STEPS, 3, 4, PAIR, BLOCK), bf16),
            pltpu.VMEM((4, PAIR, BLOCK), f32),
            pltpu.VMEM((STEPS, PAIR, 4 * BLOCK), bf16),
            pltpu.VMEM((STEPS, 3, PAIR, 4 * BLOCK), bf16),
            pltpu.VMEM((STEPS, PAIR, 4 * BLOCK), bf16),
            pltpu.VMEM((4, PAIR, BLOCK), f32),
            pltpu.VMEM((4, BLOCK, BLOCK), f32),
            pltpu.SemaphoreType.DMA((STEPS * SLOTS,)),
            pltpu.SemaphoreType.DMA((STEPS * SLOTS,)),
        ],
        compiler_params=pltpu.CompilerParams(
            collective_id=0, has_side_effects=True, vmem_limit_bytes=56 * 2**20
        ),
        name="polar_steps",
    )(density, pattern)


def solution(mesh):
    placed = (P("grid", "rep"), P())
    return jax.shard_map(
        per_device, mesh=mesh, in_specs=placed, out_specs=P("grid", "rep"), check_vma=False
    )
```

```python
import math

import jax
import jax.numpy as jnp
from jax import lax
from jax.experimental import pallas as pl
from jax.experimental.pallas import tpu as pltpu
from jax.sharding import PartitionSpec as P

BLOCK = 128
STEPS = 2
ORDER = 4096
MESH = pl.DeviceIdType.MESH
RING = 4
PAIR = 2 * BLOCK
HALF = BLOCK // 2
FAR_FIRST = (2, 1, 3)
NEAR_FIRST = (1, 3, 2)

GROUPS = ("first", "second", "step 1", "step 2", "relay", "relay again")
STEP_GROUPS = GROUPS[2:4]
ARRIVALS = 48


def nt_dot(left, right):
    return lax.dot_general(left, right, (((1,), (1,)), ((), ())), preferred_element_type=jnp.float32)


def block_of(outer, z, core):
    return outer * 8 + z * 2 + core


def kernel(density, pattern_in, out, loaded, pattern, rows_i, rows_j, send_q, got_q, own_q, square, send_c, got_c, own_c,
           unit, relay, turned, final, load_sem, store_sem, send_sem, recv_sem):
    grid_pos = lax.axis_index("grid")
    y = lax.axis_index("rep")
    x = grid_pos // 8
    z = (grid_pos // 2) % 4
    core = grid_pos % 2
    other = 1 - core

    def device(step, p, q, z_at, core_at):
        x_at, y_at = (p, q) if step == 0 else (q, p)
        return ((x_at * 4 + z_at) * 2 + core_at, y_at)

    slots = {}
    groups = {}

    def slot(*key):
        return slots.setdefault(key, len(slots))

    def copy_at(src, dst, group, at, target):
        return pltpu.make_async_remote_copy(
            src_ref=src, dst_ref=dst, send_sem=send_sem.at[group], recv_sem=recv_sem.at[at],
            device_id=target, device_id_type=MESH,
        )

    def rows(start, size):
        return pl.ds(pl.multiple_of(start, size), size)

    def turn(a, d):
        return (a + d) % RING

    barrier = pltpu.get_barrier_semaphore()
    partners = [device(0, x, y, z, other)]
    for d in (1, 2, 3):
        partners += [device(0, turn(x, d), y, z, core), device(0, x, turn(y, d), z, core),
                     device(0, x, y, turn(z, d), core), device(0, x, y, turn(z, d), other)]
    for partner in partners:
        pl.semaphore_signal(barrier, inc=1, device_id=partner, device_id_type=MESH)
    loads = [pltpu.make_async_copy(density, loaded, load_sem.at[0]), pltpu.make_async_copy(pattern_in, pattern, load_sem.at[1])]
    for load in loads:
        load.start()
    for load in loads:
        load.wait()

    def keep(row_block, col_block):
        return pattern[row_block, col_block].astype(jnp.float32)

    mine = rows(x * PAIR + core * BLOCK, BLOCK)
    for b in range(8):
        cols = pl.ds(b * BLOCK, BLOCK)
        masked = loaded[:, cols].astype(jnp.float32) * keep(block_of(x, z, core), y * 8 + b)
        rows_j[0, mine, cols] = masked.astype(jnp.bfloat16)
    pl.semaphore_wait(barrier, len(partners))

    stores = []

    def total(size):
        return rows_j.at[:, pl.ds(0, size // (2 * STEPS * rows_j.shape[2]))]

    def bytes_of(ref):
        return math.prod(ref.shape) * jnp.dtype(ref.dtype).itemsize

    def send(src, dst, target, group, *key):
        copy_at(src, dst, GROUPS.index(group), slot(*key), target).start()
        groups[group] = groups.get(group, 0) + bytes_of(src)

    def await_copy(dst, *key):
        copy_at(dst, dst, 0, slot(*key), (grid_pos, y)).wait_recv()

    def gather_first(p, q):
        sibling = device(0, p, q, z, other)

        def target(ring, d):
            return device(0, turn(p, d), q, z, core) if ring == "j" else device(0, p, q, turn(z, d), core)

        def place(ring, d, half, core_at=core):
            if ring == "j":
                return rows_j.at[0, rows(turn(p, d) * PAIR + core_at * BLOCK + half * HALF, HALF)]
            return rows_i.at[0, rows(turn(z, d) * BLOCK + half * HALF, HALF)]

        own = [rows_j.at[0, rows(p * PAIR + core * BLOCK + half * HALF, HALF)] for half in range(2)]
        for d, half in ((1, 0), (3, 1)):
            send(own[half], place("j", 0, half), target("j", d), "first", "near", "j", d)
            send(own[half], place("i", 0, half), target("i", d), "first", "near", "i", d)
        whole = rows_j.at[0, rows(p * PAIR + core * BLOCK, BLOCK)]
        send(whole, whole, sibling, "first", "pair")
        for d, half in ((1, 1), (3, 0)):
            send(own[half], place("j", 0, half), target("j", d), "first", "late", "j")
            send(own[half], place("i", 0, half), target("i", d), "first", "late", "i")
        rows_i[0, rows(z * BLOCK, BLOCK), :] = rows_j[0, rows(p * PAIR + core * BLOCK, BLOCK), :]
        await_copy(rows_j.at[0, rows(p * PAIR + other * BLOCK, BLOCK)], "pair")
        for b in range(4):
            unit[0, :, pl.ds(b * BLOCK, BLOCK)] = rows_j[0, rows(p * PAIR, PAIR), rows((2 * b + core) * BLOCK, BLOCK)]
        send_unit(0, p, q)
        for d, half in ((1, 0), (3, 1)):
            for ring in ("j", "i"):
                here = place(ring, RING - d, half)
                await_copy(here, "near", ring, d)
                send(here, here, target(ring, d), "first", *(("far", "j") if ring == "j" else ("late", "i")))
                if ring == "j":
                    send(here, here, sibling, "first", "shared")
        await_copy(total(2 * bytes_of(own[0])), "late", "j")
        for d, half in ((1, 1), (3, 0)):
            here = place("j", RING - d, half)
            send(here, here, sibling, "first", "shared")
        await_copy(total(2 * bytes_of(own[0])), "far", "j")
        for half in range(2):
            here = place("j", 2, half)
            send(here, here, sibling, "first", "shared")
        await_copy(total(4 * bytes_of(own[0])), "late", "i")
        await_copy(total(6 * bytes_of(own[0])), "shared")

    def send_unit(step, p, q):
        lag = turn(p - q, RING)
        at = slot("relay", step)

        @pl.when(lag != 0)
        def _():
            copy_at(unit.at[step], relay.at[step, lag - 1], GROUPS.index("relay") + step, at, device(step, p, p, z, core)).start()

    def pass_units_on(step, p, q):
        at, onward = slot("relay", step), slot("turned", step)

        @pl.when(p == q)
        def _():
            await_copy(relay.at[step], "relay", step)
            for d in (1, 2, 3):
                copy_at(relay.at[step, d - 1], turned.at[step], GROUPS.index("relay") + step, onward,
                        device(step, turn(p, RING - d), q, z, core)).start()
            turned[step] = unit[step]

    def await_turned(step, p, q):
        slot("turned", step)

        @pl.when(p != q)
        def _():
            await_copy(turned.at[step], "turned", step)

    def drain_units(step, p, q):
        def drain(ref):
            copy_at(ref, ref, GROUPS.index("relay") + step, 0, (grid_pos, y)).wait_send()

        pl.when(p != q)(lambda: drain(unit.at[step]))
        pl.when(p == q)(lambda: drain(relay.at[step]))

    def tile_j(p_at, chunk, core_at):
        return rows_j.at[1, rows(p_at * PAIR, PAIR), rows((2 * chunk + core_at) * BLOCK, BLOCK)]

    def tile_i(z_at, chunk, core_at):
        return rows_i.at[1, rows(z_at * BLOCK, BLOCK), rows((2 * chunk + core_at) * BLOCK, BLOCK)]

    def send_chunk(chunk, p, q):
        own = tile_j(p, chunk, core)
        for d in (1, 3):
            send(own, own, device(1, turn(p, d), q, z, core), "second", "near", chunk)
        send(own, own, device(1, p, q, z, other), "second", "shared again")
        for d in NEAR_FIRST:
            for to in (core, other):
                src = rows_j.at[1, rows(p * PAIR + to * BLOCK, BLOCK), rows((2 * chunk + core) * BLOCK, BLOCK)]
                send(src, tile_i(z, chunk, core), device(1, p, q, turn(z, d), to), "second", "slab again")
        tile_i(z, chunk, core)[...] = rows_j[1, rows(p * PAIR + core * BLOCK, BLOCK), rows((2 * chunk + core) * BLOCK, BLOCK)]

    def pass_chunk_on(chunk, p, q):
        await_copy(total(2 * bytes_of(tile_j(p, chunk, core))), "near", chunk)
        for d in (1, 3):
            here = tile_j(turn(p, RING - d), chunk, core)
            if (chunk % 2 == 0) == (d == 1):
                send(here, here, device(1, turn(p, d), q, z, core), "second", "far", chunk)
            send(here, here, device(1, p, q, z, other), "second", "shared again")

    def finish_chunk(chunk, p, q):
        here = tile_j(turn(p, 2), chunk, core)
        await_copy(here, "far", chunk)
        send(here, here, device(1, p, q, z, other), "second", "shared again")

    def await_chunks(p, q):
        await_copy(total(16 * bytes_of(tile_j(p, 0, other))), "shared again")
        for chunk in range(4):
            tile_i(z, chunk, other)[...] = rows_j[1, rows(p * PAIR + core * BLOCK, BLOCK), rows((2 * chunk + other) * BLOCK, BLOCK)]
        await_copy(total(24 * bytes_of(tile_i(z, 0, core))), "slab again")

    def square_terms(step, p, q):
        for half in range(2):
            lines = pl.ds(half * PAIR, PAIR)
            left = rows_i[step, lines, :]
            for d in FAR_FIRST:
                send_q[step, d - 1, lines, :] = nt_dot(left, rows_j[step, rows(turn(q, d) * PAIR, PAIR), :]).astype(jnp.bfloat16)
            for chunk in (2 * half, 2 * half + 1):
                part = pl.ds(chunk * BLOCK, BLOCK)
                for d in FAR_FIRST:
                    send(send_q.at[step, d - 1, part], got_q.at[step, d - 1, part], device(step, p, turn(q, d), z, core),
                         STEP_GROUPS[step], "q", step, chunk)
            own_q[lines, :] = nt_dot(left, rows_j[step, rows(q * PAIR, PAIR), :])

    def add_square(step, p, q, chunk):
        part = pl.ds(chunk * BLOCK, BLOCK)
        await_copy(got_q.at[step, :, part], "q", step, chunk)
        terms = own_q[part, :]
        for d in FAR_FIRST:
            terms += got_q[step, d - 1, part, :].astype(jnp.float32)
        for b in range(2):
            scale = keep(block_of(p, chunk, core), block_of(q, z, b)) * (1.0 / ORDER)
            square[step, part, rows(z * PAIR + b * BLOCK, BLOCK)] = (
                terms[:, b * BLOCK:(b + 1) * BLOCK] * scale).astype(jnp.bfloat16)
        block = square.at[step, part, rows(z * PAIR, PAIR)]
        for d in NEAR_FIRST:
            send(block, block, device(step, p, q, turn(z, d), core), STEP_GROUPS[step], "r", step, chunk)

    def cubic_terms(step, p, q, chunk):
        part = pl.ds(chunk * BLOCK, BLOCK)
        await_copy(got_q.at[step, :, part], "r", step, chunk)
        right = square[step, part, :]
        for d in FAR_FIRST:
            send_c[step, d - 1, chunk] = nt_dot(rows_j[step, rows(turn(q, d) * PAIR, PAIR), :], right).astype(jnp.bfloat16)
            send(send_c.at[step, d - 1, chunk], got_c.at[step, d - 1, chunk], device(step, p, turn(q, d), z, core),
                 STEP_GROUPS[step], "c", step, chunk)
        own_c[chunk] = nt_dot(rows_j[step, rows(q * PAIR, PAIR), :], right)

    def add_cubic(step, p, q, chunk):
        await_copy(got_c.at[step, :, chunk], "c", step, chunk)
        terms = own_c[chunk]
        for d in FAR_FIRST:
            terms += got_c[step, d - 1, chunk].astype(jnp.float32)
        cols = pl.ds(chunk * BLOCK, BLOCK)
        updated = 1.5 * turned[step, :, cols].astype(jnp.float32) - 0.5 * terms
        for b in range(2):
            part = updated[b * BLOCK:(b + 1) * BLOCK] * keep(block_of(q, z, b), block_of(p, chunk, core))
            if step == 0:
                unit[1, pl.ds(b * BLOCK, BLOCK), cols] = part.astype(jnp.bfloat16)
            else:
                final[chunk, pl.ds(b * BLOCK, BLOCK), :] = part
        if step == 0:
            tile_j(q, chunk, core)[...] = unit[1, :, cols]
            send_chunk(chunk, q, p)
        else:
            place = out.at[:, rows((2 * chunk + core) * BLOCK, BLOCK)]
            send(final.at[chunk, rows(other * BLOCK, BLOCK)], place, device(step, p, q, z, other), STEP_GROUPS[step], "f")
            store = pltpu.make_async_copy(final.at[chunk, rows(core * BLOCK, BLOCK)], place, store_sem.at[chunk])
            store.start()
            stores.append(store)

    for step in range(STEPS):
        p, q = (x, y) if step == 0 else (y, x)
        at = (step, p, q)
        if step == 0:
            gather_first(p, q)
        else:
            send_unit(*at)
            finish_chunk(0, p, q)
            pass_chunk_on(2, p, q)
            finish_chunk(1, p, q)
            pass_chunk_on(3, p, q)
            finish_chunk(2, p, q)
            finish_chunk(3, p, q)
            await_chunks(p, q)
        square_terms(*at)
        pass_units_on(*at)
        add_square(*at, 0)
        add_square(*at, 1)
        add_square(*at, 2)
        cubic_terms(*at, 0)
        add_square(*at, 3)
        cubic_terms(*at, 1)
        cubic_terms(*at, 2)
        await_turned(*at)
        add_cubic(*at, 0)
        cubic_terms(*at, 3)
        add_cubic(*at, 1)
        if step == 0:
            pass_chunk_on(0, q, p)
        add_cubic(*at, 2)
        if step == 0:
            pass_chunk_on(1, q, p)
        add_cubic(*at, 3)

    await_copy(final.at[:, pl.ds(0, BLOCK)], "f")
    for group, size in groups.items():
        copy_at(total(size), total(size), GROUPS.index(group), 0, (grid_pos, y)).wait_send()
    for store in stores:
        store.wait()
    assert len(slots) == ARRIVALS, len(slots)
    for step in range(STEPS):
        p, q = (x, y) if step == 0 else (y, x)
        drain_units(step, p, q)


def per_device(density, pattern):
    bf16, f32 = jnp.bfloat16, jnp.float32
    quarter = ORDER // RING
    return pl.pallas_call(
        kernel,
        out_shape=jax.ShapeDtypeStruct(density.shape, f32),
        in_specs=[pl.BlockSpec(memory_space=pl.ANY)] * 2,
        out_specs=pl.BlockSpec(memory_space=pl.ANY),
        scratch_shapes=[
            pltpu.VMEM(density.shape, bf16),
            pltpu.SMEM(pattern.shape, jnp.int32),
            pltpu.VMEM((STEPS, 4 * BLOCK, quarter), bf16),
            pltpu.VMEM((STEPS, 8 * BLOCK, quarter), bf16),
            pltpu.VMEM((STEPS, 3, 4 * BLOCK, PAIR), bf16),
            pltpu.VMEM((STEPS, 3, 4 * BLOCK, PAIR), bf16),
            pltpu.VMEM((4 * BLOCK, PAIR), f32),
            pltpu.VMEM((STEPS, 4 * BLOCK, quarter), bf16),
            pltpu.VMEM((STEPS, 3, 4, PAIR, BLOCK), bf16),
            pltpu.VMEM((STEPS, 3, 4, PAIR, BLOCK), bf16),
            pltpu.VMEM((4, PAIR, BLOCK), f32),
            pltpu.VMEM((STEPS, PAIR, 4 * BLOCK), bf16),
            pltpu.VMEM((STEPS, 3, PAIR, 4 * BLOCK), bf16),
            pltpu.VMEM((STEPS, PAIR, 4 * BLOCK), bf16),
            pltpu.VMEM((4, PAIR, BLOCK), f32),
            pltpu.SemaphoreType.DMA((2,)),
            pltpu.SemaphoreType.DMA((4,)),
            pltpu.SemaphoreType.DMA((len(GROUPS),)),
            pltpu.SemaphoreType.DMA((ARRIVALS,)),
        ],
        compiler_params=pltpu.CompilerParams(
            collective_id=0, has_side_effects=True, vmem_limit_bytes=56 * 2**20
        ),
        name="polar_steps",
    )(density, pattern)


def solution(mesh):
    placed = (P("grid", "rep"), P())
    return jax.shard_map(
        per_device, mesh=mesh, in_specs=placed, out_specs=P("grid", "rep"), check_vma=False
    )
```

```python
import math

import jax
import jax.numpy as jnp
from jax import lax
from jax.experimental import pallas as pl
from jax.experimental.pallas import tpu as pltpu
from jax.sharding import PartitionSpec as P

BLOCK = 128
STEPS = 2
ORDER = 4096
MESH = pl.DeviceIdType.MESH
RING = 4
PAIR = 2 * BLOCK
HALF = BLOCK // 2
FAR_FIRST = (2, 1, 3)
NEAR_FIRST = (1, 3, 2)

GROUPS = ("first", "second", "step 1", "step 2", "relay", "relay again")
STEP_GROUPS = GROUPS[2:4]
MERGED = ((0, 0), (0, 1), (0, 2), (0, 3))
ARRIVALS = 56 + len(MERGED)
DIRECT = (2, 3)


def nt_dot(left, right):
    return lax.dot_general(left, right, (((1,), (1,)), ((), ())), preferred_element_type=jnp.float32)


def block_of(outer, z, core):
    return outer * 8 + z * 2 + core


def kernel(density, pattern_in, out, loaded, pattern, rows_i, rows_j, send_q, got_q, terms_q, square, send_c, got_c, terms_c, passing,
           unit, relay, turned, final, load_sem, send_sem, recv_sem):
    grid_pos = lax.axis_index("grid")
    y = lax.axis_index("rep")
    x = grid_pos // 8
    z = (grid_pos // 2) % 4
    core = grid_pos % 2
    other = 1 - core

    def device(step, p, q, z_at, core_at):
        x_at, y_at = (p, q) if step == 0 else (q, p)
        return ((x_at * 4 + z_at) * 2 + core_at, y_at)

    slots = {}
    groups = {}

    def slot(*key):
        return slots.setdefault(key, len(slots))

    def copy_at(src, dst, group, at, target):
        return pltpu.make_async_remote_copy(
            src_ref=src, dst_ref=dst, send_sem=send_sem.at[group], recv_sem=recv_sem.at[at],
            device_id=target, device_id_type=MESH,
        )

    def rows(start, size):
        return pl.ds(pl.multiple_of(start, size), size)

    def turn(a, d):
        return (a + d) % RING

    barrier = pltpu.get_barrier_semaphore()
    partners = [device(0, x, y, z, other)]
    for d in (1, 2, 3):
        partners += [device(0, turn(x, d), y, z, core), device(0, x, turn(y, d), z, core),
                     device(0, x, y, turn(z, d), core), device(0, x, y, turn(z, d), other)]
    for partner in partners:
        pl.semaphore_signal(barrier, inc=1, device_id=partner, device_id_type=MESH)
    loads = [pltpu.make_async_copy(density, loaded, load_sem.at[0]), pltpu.make_async_copy(pattern_in, pattern, load_sem.at[1])]
    for load in loads:
        load.start()
    for load in loads:
        load.wait()

    def keep(row_block, col_block):
        return pattern[row_block, col_block].astype(jnp.float32)

    mine = rows(x * PAIR + core * BLOCK, BLOCK)
    for b in range(8):
        cols = pl.ds(b * BLOCK, BLOCK)
        masked = loaded[:, cols].astype(jnp.float32) * keep(block_of(x, z, core), y * 8 + b)
        rows_j[0, mine, cols] = masked.astype(jnp.bfloat16)
    pl.semaphore_wait(barrier, len(partners))

    def total(size):
        return rows_j.at[:, pl.ds(0, size // (2 * STEPS * rows_j.shape[2]))]

    def bytes_of(ref):
        return math.prod(ref.shape) * jnp.dtype(ref.dtype).itemsize

    def send(src, dst, target, group, *key):
        copy_at(src, dst, GROUPS.index(group), slot(*key), target).start()
        groups[group] = groups.get(group, 0) + bytes_of(src)

    def await_copy(dst, *key):
        copy_at(dst, dst, 0, slot(*key), (grid_pos, y)).wait_recv()

    def gather_first(p, q):
        sibling = device(0, p, q, z, other)

        def target(ring, d):
            return device(0, turn(p, d), q, z, core) if ring == "j" else device(0, p, q, turn(z, d), core)

        def place(ring, d, half, core_at=core):
            if ring == "j":
                return rows_j.at[0, rows(turn(p, d) * PAIR + core_at * BLOCK + half * HALF, HALF)]
            return rows_i.at[0, rows(turn(z, d) * BLOCK + half * HALF, HALF)]

        own = [rows_j.at[0, rows(p * PAIR + core * BLOCK + half * HALF, HALF)] for half in range(2)]
        for d, half in ((1, 0), (3, 1)):
            send(own[half], place("j", 0, half), target("j", d), "first", "near", "j", d)
            send(own[half], place("i", 0, half), target("i", d), "first", "near", "i", d)
        whole = rows_j.at[0, rows(p * PAIR + core * BLOCK, BLOCK)]
        send(whole, whole, sibling, "first", "pair")
        for d, half in ((1, 1), (3, 0)):
            send(own[half], place("j", 0, half), target("j", d), "first", "late", "j")
            send(own[half], place("i", 0, half), target("i", d), "first", "late", "i")
        rows_i[0, rows(z * BLOCK, BLOCK), :] = rows_j[0, rows(p * PAIR + core * BLOCK, BLOCK), :]
        await_copy(rows_j.at[0, rows(p * PAIR + other * BLOCK, BLOCK)], "pair")
        for b in range(4):
            unit[0, :, pl.ds(b * BLOCK, BLOCK)] = rows_j[0, rows(p * PAIR, PAIR), rows((2 * b + core) * BLOCK, BLOCK)]
        send_unit(0, p, q, pl.ds(0, 4 * BLOCK))
        for d, half in ((1, 0), (3, 1)):
            for ring in ("j", "i"):
                here = place(ring, RING - d, half)
                await_copy(here, "near", ring, d)
                send(here, here, target(ring, d), "first", *(("far", "j") if ring == "j" else ("late", "i")))
                if ring == "j":
                    send(here, here, sibling, "first", "shared")
        await_copy(total(2 * bytes_of(own[0])), "late", "j")
        for d, half in ((1, 1), (3, 0)):
            here = place("j", RING - d, half)
            send(here, here, sibling, "first", "shared")
        await_copy(total(2 * bytes_of(own[0])), "far", "j")
        for half in range(2):
            here = place("j", 2, half)
            send(here, here, sibling, "first", "shared")
        await_copy(total(4 * bytes_of(own[0])), "late", "i")
        await_copy(total(6 * bytes_of(own[0])), "shared")

    def send_unit(step, p, q, cols):
        lag = turn(p - q, RING)
        at = slot("relay", step)

        @pl.when(lag != 0)
        def _():
            copy_at(unit.at[step, :, cols], relay.at[step, lag - 1, :, cols], GROUPS.index("relay") + step, at,
                    device(step, p, p, z, core)).start()

    def pass_units_on(step, p, q):
        at, onward = slot("relay", step), slot("turned", step)

        @pl.when(p == q)
        def _():
            await_copy(relay.at[step], "relay", step)
            for d in (1, 2, 3):
                copy_at(relay.at[step, d - 1], turned.at[step], GROUPS.index("relay") + step, onward,
                        device(step, turn(p, RING - d), q, z, core)).start()
            turned[step] = unit[step]

    def await_turned(step, p, q):
        slot("turned", step)

        @pl.when(p != q)
        def _():
            await_copy(turned.at[step], "turned", step)

    def drain_units(step, p, q):
        def drain(ref):
            copy_at(ref, ref, GROUPS.index("relay") + step, 0, (grid_pos, y)).wait_send()

        pl.when(p != q)(lambda: drain(unit.at[step]))
        pl.when(p == q)(lambda: drain(relay.at[step]))

    def tile_j(p_at, chunk, core_at):
        return rows_j.at[1, rows(p_at * PAIR, PAIR), rows((2 * chunk + core_at) * BLOCK, BLOCK)]

    def tile_i(z_at, chunk, core_at):
        return rows_i.at[1, rows(z_at * BLOCK, BLOCK), rows((2 * chunk + core_at) * BLOCK, BLOCK)]

    def send_chunk(chunk, p, q):
        own = tile_j(p, chunk, core)
        for d in (1, 3):
            send(own, own, device(1, turn(p, d), q, z, core), "second", "near", chunk)
        if chunk in DIRECT:
            send(own, own, device(1, turn(p, 2), q, z, core), "second", "far", chunk)
        send(own, own, device(1, p, q, z, other), "second", "shared again")
        for d in NEAR_FIRST:
            for to in (core, other):
                src = rows_j.at[1, rows(p * PAIR + to * BLOCK, BLOCK), rows((2 * chunk + core) * BLOCK, BLOCK)]
                send(src, tile_i(z, chunk, core), device(1, p, q, turn(z, d), to), "second", "slab again")
        tile_i(z, chunk, core)[...] = rows_j[1, rows(p * PAIR + core * BLOCK, BLOCK), rows((2 * chunk + core) * BLOCK, BLOCK)]

    def pass_chunk_on(chunk, p, q):
        await_copy(total(2 * bytes_of(tile_j(p, chunk, core))), "near", chunk)
        for d in (1, 3):
            here = tile_j(turn(p, RING - d), chunk, core)
            if chunk not in DIRECT and (chunk % 2 == 0) == (d == 1):
                send(here, here, device(1, turn(p, d), q, z, core), "second", "far", chunk)
            send(here, here, device(1, p, q, z, other), "second", "shared again")

    def finish_chunk(chunk, p, q):
        here = tile_j(turn(p, 2), chunk, core)
        await_copy(here, "far", chunk)
        send(here, here, device(1, p, q, z, other), "second", "shared again")

    def await_chunks(p, q):
        await_copy(total(16 * bytes_of(tile_j(p, 0, other))), "shared again")
        for chunk in range(4):
            tile_i(z, chunk, other)[...] = rows_j[1, rows(p * PAIR + core * BLOCK, BLOCK), rows((2 * chunk + other) * BLOCK, BLOCK)]
        await_copy(total(24 * bytes_of(tile_i(z, 0, core))), "slab again")

    def square_terms(step, p, q):
        for half in range(2):
            lines = pl.ds(half * PAIR, PAIR)
            terms_q[lines, :] = nt_dot(rows_i[step, lines, :], rows_j[step])
            send_q[step, lines, :] = terms_q[lines, :].astype(jnp.bfloat16)
            for strip in range(4 * half, 4 * half + 4):
                part = pl.ds(strip * HALF, HALF)
                for d in FAR_FIRST:
                    send(send_q.at[step, part, rows(turn(q, d) * PAIR, PAIR)], got_q.at[step, d - 1, part],
                         device(step, p, turn(q, d), z, core), STEP_GROUPS[step], "q", step, strip)

    def add_square(step, p, q, strip):
        part = pl.ds(strip * HALF, HALF)
        await_copy(got_q.at[step, :, part], "q", step, strip)
        terms = terms_q[part, rows(q * PAIR, PAIR)]
        for d in FAR_FIRST:
            terms += got_q[step, d - 1, part, :].astype(jnp.float32)
        for b in range(2):
            scale = keep(block_of(p, strip // 2, core), block_of(q, z, b)) * (1.0 / ORDER)
            square[step, part, rows(z * PAIR + b * BLOCK, BLOCK)] = (
                terms[:, b * BLOCK:(b + 1) * BLOCK] * scale).astype(jnp.bfloat16)
        block = square.at[step, part, rows(z * PAIR, PAIR)]
        for d in NEAR_FIRST:
            send(block, block, device(step, p, q, turn(z, d), core), STEP_GROUPS[step], "r", step, strip // 2)

    def cubic_terms(step, p, q, chunk):
        part = pl.ds(chunk * BLOCK, BLOCK)
        await_copy(got_q.at[step, :, part], "r", step, chunk)
        for b in range(2):
            lines = pl.ds(b * 512, 512)
            terms_c[chunk, lines] = nt_dot(rows_j[step, lines, :], square[step, part, :])
            send_c[step, chunk, lines] = terms_c[chunk, lines].astype(jnp.bfloat16)
        if (step, chunk) in MERGED:
            for b, d in enumerate((1, 3)):
                send(send_c.at[step, chunk, rows(turn(q, 2) * PAIR + b * BLOCK, BLOCK)], passing.at[chunk, b],
                     device(step, p, turn(q, d), z, core), STEP_GROUPS[step], "via", step, chunk)
            for b, d in enumerate((1, 3)):
                send_cubic(step, p, q, chunk, 1 - b, d)
        else:
            for d in FAR_FIRST:
                send(send_c.at[step, chunk, rows(turn(q, d) * PAIR, PAIR)], got_c.at[step, d - 1, chunk],
                     device(step, p, turn(q, d), z, core), STEP_GROUPS[step], "c", step, chunk)

    def send_cubic(step, p, q, chunk, b, d):
        send(send_c.at[step, chunk, rows(turn(q, d) * PAIR + b * BLOCK, BLOCK)],
             got_c.at[step, d - 1, chunk, pl.ds(b * BLOCK, BLOCK)],
             device(step, p, turn(q, d), z, core), STEP_GROUPS[step], "c", step, chunk)

    def merge_terms(step, p, q, chunk):
        if (step, chunk) not in MERGED:
            return
        await_copy(passing.at[chunk], "via", step, chunk)
        for b, d in enumerate((1, 3)):
            half = rows(turn(q, d) * PAIR + b * BLOCK, BLOCK)
            send_c[step, chunk, half, :] = (terms_c[chunk, half, :] + passing[chunk, b].astype(jnp.float32)).astype(jnp.bfloat16)
            send_cubic(step, p, q, chunk, b, d)

    def add_cubic(step, p, q, chunk):
        sources = (1, 3) if (step, chunk) in MERGED else FAR_FIRST
        await_copy(got_c.at[step, pl.ds(0, len(sources)), chunk], "c", step, chunk)
        terms = terms_c[chunk, rows(q * PAIR, PAIR), :]
        for d in sources:
            terms += got_c[step, d - 1, chunk].astype(jnp.float32)
        cols = pl.ds(chunk * BLOCK, BLOCK)
        updated = 1.5 * turned[step, :, cols].astype(jnp.float32) - 0.5 * terms
        for b in range(2):
            part = updated[b * BLOCK:(b + 1) * BLOCK] * keep(block_of(q, z, b), block_of(p, chunk, core))
            if step == 0:
                unit[1, pl.ds(b * BLOCK, BLOCK), cols] = part.astype(jnp.bfloat16)
            else:
                final[chunk, pl.ds(b * BLOCK, BLOCK), :] = part
        if step == 0:
            tile_j(q, chunk, core)[...] = unit[1, :, cols]
            send_chunk(chunk, q, p)
            send_unit(1, q, p, cols)
        else:
            place = out.at[:, rows((2 * chunk + core) * BLOCK, BLOCK)]
            send(final.at[chunk, rows(other * BLOCK, BLOCK)], place, device(step, p, q, z, other), STEP_GROUPS[step], "f")
            place[...] = final[chunk, rows(core * BLOCK, BLOCK), :]

    for step in range(STEPS):
        p, q = (x, y) if step == 0 else (y, x)
        at = (step, p, q)
        if step == 0:
            gather_first(p, q)
        else:
            finish_chunk(0, p, q)
            pass_chunk_on(2, p, q)
            finish_chunk(1, p, q)
            pass_chunk_on(3, p, q)
            finish_chunk(2, p, q)
            finish_chunk(3, p, q)
            pass_units_on(*at)
            await_chunks(p, q)
        square_terms(*at)
        for strip in range(5):
            add_square(*at, strip)
            if strip == 0 and step == 0:
                pass_units_on(*at)
        cubic_terms(*at, 0)
        add_square(*at, 5)
        add_square(*at, 6)
        cubic_terms(*at, 1)
        merge_terms(*at, 0)
        add_square(*at, 7)
        cubic_terms(*at, 2)
        merge_terms(*at, 1)
        await_turned(*at)
        add_cubic(*at, 0)
        cubic_terms(*at, 3)
        merge_terms(*at, 2)
        add_cubic(*at, 1)
        merge_terms(*at, 3)
        if step == 0:
            pass_chunk_on(0, q, p)
        add_cubic(*at, 2)
        if step == 0:
            pass_chunk_on(1, q, p)
        add_cubic(*at, 3)

    await_copy(final.at[:, pl.ds(0, BLOCK)], "f")
    for group, size in groups.items():
        copy_at(total(size), total(size), GROUPS.index(group), 0, (grid_pos, y)).wait_send()
    assert len(slots) == ARRIVALS, len(slots)
    for step in range(STEPS):
        p, q = (x, y) if step == 0 else (y, x)
        drain_units(step, p, q)


def per_device(density, pattern):
    bf16, f32 = jnp.bfloat16, jnp.float32
    quarter = ORDER // RING
    return pl.pallas_call(
        kernel,
        out_shape=pltpu.VMEM(density.shape, f32),
        in_specs=[pl.BlockSpec(memory_space=pl.ANY)] * 2,
        out_specs=pl.BlockSpec(memory_space=pltpu.VMEM),
        scratch_shapes=[
            pltpu.VMEM(density.shape, bf16),
            pltpu.SMEM(pattern.shape, jnp.int32),
            pltpu.VMEM((STEPS, 4 * BLOCK, quarter), bf16),
            pltpu.VMEM((STEPS, 8 * BLOCK, quarter), bf16),
            pltpu.VMEM((STEPS, 4 * BLOCK, quarter), bf16),
            pltpu.VMEM((STEPS, 3, 4 * BLOCK, PAIR), bf16),
            pltpu.VMEM((4 * BLOCK, quarter), f32),
            pltpu.VMEM((STEPS, 4 * BLOCK, quarter), bf16),
            pltpu.VMEM((STEPS, 4, quarter, BLOCK), bf16),
            pltpu.VMEM((STEPS, 3, 4, PAIR, BLOCK), bf16),
            pltpu.VMEM((4, quarter, BLOCK), f32),
            pltpu.VMEM((4, 2, BLOCK, BLOCK), bf16),
            pltpu.VMEM((STEPS, PAIR, 4 * BLOCK), bf16),
            pltpu.VMEM((STEPS, 3, PAIR, 4 * BLOCK), bf16),
            pltpu.VMEM((STEPS, PAIR, 4 * BLOCK), bf16),
            pltpu.VMEM((4, PAIR, BLOCK), f32),
            pltpu.SemaphoreType.DMA((2,)),
            pltpu.SemaphoreType.DMA((len(GROUPS),)),
            pltpu.SemaphoreType.DMA((ARRIVALS,)),
        ],
        compiler_params=pltpu.CompilerParams(
            collective_id=0, has_side_effects=True, vmem_limit_bytes=56 * 2**20
        ),
        name="polar_steps",
    )(density, pattern)


def solution(mesh):
    placed = (P("grid", "rep"), P())
    return jax.shard_map(
        per_device, mesh=mesh, in_specs=placed, out_specs=P("grid", "rep"), check_vma=False
    )
```

```python
import math

import jax
import jax.numpy as jnp
from jax import lax
from jax.experimental import pallas as pl
from jax.experimental.pallas import tpu as pltpu
from jax.sharding import PartitionSpec as P

BLOCK = 128
STEPS = 2
ORDER = 4096
MESH = pl.DeviceIdType.MESH
RING = 4
PAIR = 2 * BLOCK
HALF = BLOCK // 2
FAR_FIRST = (2, 1, 3)
NEAR_FIRST = (1, 3, 2)

GROUPS = ("first", "second", "step 1", "step 2", "relay", "relay again")
STEP_GROUPS = GROUPS[2:4]
MERGED = ((0, 0), (0, 1), (0, 2), (0, 3))
ARRIVALS = 66 + len(MERGED)
DIRECT = (2, 3)


def nt_dot(left, right):
    return lax.dot_general(left, right, (((1,), (1,)), ((), ())), preferred_element_type=jnp.float32)


def block_of(outer, z, core):
    return outer * 8 + z * 2 + core


def kernel(density, pattern_in, out, loaded, pattern, rows_i, rows_j, send_q, got_q, terms_q, square, send_c, got_c, terms_c, passing, got_f, got_own, turned_rest,
           unit, relay, turned, load_sem, send_sem, recv_sem):
    grid_pos = lax.axis_index("grid")
    y = lax.axis_index("rep")
    x = grid_pos // 8
    z = (grid_pos // 2) % 4
    core = grid_pos % 2
    other = 1 - core

    def device(step, p, q, z_at, core_at):
        x_at, y_at = (p, q) if step == 0 else (q, p)
        return ((x_at * 4 + z_at) * 2 + core_at, y_at)

    slots = {}
    groups = {}

    def slot(*key):
        return slots.setdefault(key, len(slots))

    def copy_at(src, dst, group, at, target):
        return pltpu.make_async_remote_copy(
            src_ref=src, dst_ref=dst, send_sem=send_sem.at[group], recv_sem=recv_sem.at[at],
            device_id=target, device_id_type=MESH,
        )

    def rows(start, size):
        return pl.ds(pl.multiple_of(start, size), size)

    def turn(a, d):
        return (a + d) % RING

    barrier = pltpu.get_barrier_semaphore()
    partners = [device(0, x, y, z, other)]
    for d in (1, 2, 3):
        partners += [device(0, turn(x, d), y, z, core), device(0, turn(x, d), y, z, other), device(0, x, turn(y, d), z, core),
                     device(0, x, y, turn(z, d), core), device(0, x, y, turn(z, d), other)]
    for partner in partners:
        pl.semaphore_signal(barrier, inc=1, device_id=partner, device_id_type=MESH)
    loads = [pltpu.make_async_copy(density, loaded, load_sem.at[0]), pltpu.make_async_copy(pattern_in, pattern, load_sem.at[1])]
    for load in loads:
        load.start()
    for load in loads:
        load.wait()

    def keep(row_block, col_block):
        return pattern[row_block, col_block].astype(jnp.float32)

    mine = rows(x * PAIR + core * BLOCK, BLOCK)
    for b in range(8):
        cols = pl.ds(b * BLOCK, BLOCK)
        masked = loaded[:, cols].astype(jnp.float32) * keep(block_of(x, z, core), y * 8 + b)
        rows_j[0, mine, cols] = masked.astype(jnp.bfloat16)
    pl.semaphore_wait(barrier, len(partners))

    def total(size):
        return rows_j.at[:, pl.ds(0, size // (2 * STEPS * rows_j.shape[2]))]

    def bytes_of(ref):
        return math.prod(ref.shape) * jnp.dtype(ref.dtype).itemsize

    def send(src, dst, target, group, *key):
        copy_at(src, dst, GROUPS.index(group), slot(*key), target).start()
        groups[group] = groups.get(group, 0) + bytes_of(src)

    def await_copy(dst, *key):
        copy_at(dst, dst, 0, slot(*key), (grid_pos, y)).wait_recv()

    def gather_first(p, q):
        sibling = device(0, p, q, z, other)

        def target(ring, d):
            return device(0, turn(p, d), q, z, core) if ring == "j" else device(0, p, q, turn(z, d), core)

        def place(ring, d, half, core_at=core):
            if ring == "j":
                return rows_j.at[0, rows(turn(p, d) * PAIR + core_at * BLOCK + half * HALF, HALF)]
            return rows_i.at[0, rows(turn(z, d) * BLOCK + half * HALF, HALF)]

        own = [rows_j.at[0, rows(p * PAIR + core * BLOCK + half * HALF, HALF)] for half in range(2)]
        for d, half in ((1, 0), (3, 1)):
            send(own[half], place("j", 0, half), target("j", d), "first", "near", "j", d)
            send(own[half], place("i", 0, half), target("i", d), "first", "near", "i", d)
        whole = rows_j.at[0, rows(p * PAIR + core * BLOCK, BLOCK)]
        send(whole, whole, sibling, "first", "pair")
        for d, half in ((1, 1), (3, 0)):
            send(own[half], place("j", 0, half), target("j", d), "first", "late", "j")
            send(own[half], place("i", 0, half), target("i", d), "first", "late", "i")
        rows_i[0, rows(z * BLOCK, BLOCK), :] = rows_j[0, rows(p * PAIR + core * BLOCK, BLOCK), :]
        await_copy(rows_j.at[0, rows(p * PAIR + other * BLOCK, BLOCK)], "pair")
        for b in range(4):
            unit[0, :, pl.ds(b * BLOCK, BLOCK)] = rows_j[0, rows(p * PAIR, PAIR), rows((2 * b + core) * BLOCK, BLOCK)]
        send_unit(0, p, q, pl.ds(0, 4 * BLOCK))
        for d, half in ((1, 0), (3, 1)):
            for ring in ("j", "i"):
                here = place(ring, RING - d, half)
                await_copy(here, "near", ring, d)
                send(here, here, target(ring, d), "first", *(("far", "j") if ring == "j" else ("late", "i")))
                if ring == "j":
                    send(here, here, sibling, "first", "shared")
        await_copy(total(2 * bytes_of(own[0])), "late", "j")
        for d, half in ((1, 1), (3, 0)):
            here = place("j", RING - d, half)
            send(here, here, sibling, "first", "shared")
        await_copy(total(2 * bytes_of(own[0])), "far", "j")
        for half in range(2):
            here = place("j", 2, half)
            send(here, here, sibling, "first", "shared")
        await_copy(total(4 * bytes_of(own[0])), "late", "i")
        await_copy(total(6 * bytes_of(own[0])), "shared")

    def send_unit(step, p, q, cols):
        lag = turn(p - q, RING)
        at = slot("relay", step)

        @pl.when(lag != 0)
        def _():
            copy_at(unit.at[step, :, cols], relay.at[step, lag - 1, :, cols], GROUPS.index("relay") + step, at,
                    device(step, p, p, z, core)).start()

    def pass_units_on(step, p, q):
        at, onward = slot("relay", step), slot("turned", step)

        @pl.when(p == q)
        def _():
            await_copy(relay.at[step], "relay", step)
            for d in (1, 2, 3):
                copy_at(relay.at[step, d - 1], turned.at[step], GROUPS.index("relay") + step, onward,
                        device(step, turn(p, RING - d), q, z, core)).start()
            turned[step] = unit[step]

    def await_turned(step, p, q):
        slot("turned", step)

        @pl.when(p != q)
        def _():
            await_copy(turned.at[step], "turned", step)

    def drain_units(step, p, q):
        def drain(ref):
            copy_at(ref, ref, GROUPS.index("relay") + step, 0, (grid_pos, y)).wait_send()

        pl.when(p != q)(lambda: drain(unit.at[step]))
        pl.when(p == q)(lambda: drain(relay.at[step]))

    def tile_j(p_at, chunk, core_at):
        return rows_j.at[1, rows(p_at * PAIR, PAIR), rows((2 * chunk + core_at) * BLOCK, BLOCK)]

    def tile_i(z_at, chunk, core_at):
        return rows_i.at[1, rows(z_at * BLOCK, BLOCK), rows((2 * chunk + core_at) * BLOCK, BLOCK)]

    def send_chunk(chunk, p, q):
        own = tile_j(p, chunk, core)
        if chunk in DIRECT:
            send(own, own, device(1, turn(p, 2), q, z, core), "second", "far", chunk)
        for d in (1, 3):
            send(own, own, device(1, turn(p, d), q, z, core), "second", "near", chunk)
        send(own, own, device(1, p, q, z, other), "second", "shared again", chunk)
        for d in NEAR_FIRST:
            for to in (core, other):
                src = rows_j.at[1, rows(p * PAIR + to * BLOCK, BLOCK), rows((2 * chunk + core) * BLOCK, BLOCK)]
                send(src, tile_i(z, chunk, core), device(1, p, q, turn(z, d), to), "second", "slab again", chunk)
        tile_i(z, chunk, core)[...] = rows_j[1, rows(p * PAIR + core * BLOCK, BLOCK), rows((2 * chunk + core) * BLOCK, BLOCK)]

    def pass_chunk_on(chunk, p, q):
        await_copy(total(2 * bytes_of(tile_j(p, chunk, core))), "near", chunk)
        for d in (1, 3):
            here = tile_j(turn(p, RING - d), chunk, core)
            if chunk not in DIRECT and (chunk % 2 == 0) == (d == 1):
                send(here, here, device(1, turn(p, d), q, z, core), "second", "far", chunk)
            send(here, here, device(1, p, q, z, other), "second", "shared again", chunk)

    def finish_chunk(chunk, p, q):
        here = tile_j(turn(p, 2), chunk, core)
        await_copy(here, "far", chunk)
        send(here, here, device(1, p, q, z, other), "second", "shared again", chunk)

    def await_chunk(chunk, p, q):
        await_copy(total(4 * bytes_of(tile_j(p, 0, other))), "shared again", chunk)
        tile_i(z, chunk, other)[...] = rows_j[1, rows(p * PAIR + core * BLOCK, BLOCK), rows((2 * chunk + other) * BLOCK, BLOCK)]
        await_copy(total(6 * bytes_of(tile_i(z, 0, core))), "slab again", chunk)

    def square_terms(step, p, q):
        for half in range(2):
            lines = pl.ds(half * PAIR, PAIR)
            terms_q[lines, :] = nt_dot(rows_i[step, lines, :], rows_j[step])
            send_q[step, lines, :] = terms_q[lines, :].astype(jnp.bfloat16)
            for strip in range(4 * half, 4 * half + 4):
                part = pl.ds(strip * HALF, HALF)
                for d in FAR_FIRST:
                    send(send_q.at[step, part, rows(turn(q, d) * PAIR, PAIR)], got_q.at[step, d - 1, part],
                         device(step, p, turn(q, d), z, core), STEP_GROUPS[step], "q", step, strip)

    def add_square(step, p, q, strip):
        part = pl.ds(strip * HALF, HALF)
        await_copy(got_q.at[step, :, part], "q", step, strip)
        terms = terms_q[part, rows(q * PAIR, PAIR)]
        for d in FAR_FIRST:
            terms += got_q[step, d - 1, part, :].astype(jnp.float32)
        for b in range(2):
            scale = keep(block_of(p, strip // 2, core), block_of(q, z, b)) * (1.0 / ORDER)
            square[step, part, rows(z * PAIR + b * BLOCK, BLOCK)] = (
                terms[:, b * BLOCK:(b + 1) * BLOCK] * scale).astype(jnp.bfloat16)
        block = square.at[step, part, rows(z * PAIR, PAIR)]
        for d in NEAR_FIRST:
            send(block, block, device(step, p, q, turn(z, d), core), STEP_GROUPS[step], "r", step, strip // 2)

    def cubic_terms(step, p, q, chunk):
        part = pl.ds(chunk * BLOCK, BLOCK)
        await_copy(got_q.at[step, :, part], "r", step, chunk)
        for b in range(4):
            lines = pl.ds(b * PAIR, PAIR)
            terms_c[chunk, lines] = nt_dot(rows_j[step, lines, :], square[step, part, :])
            send_c[step, chunk, lines] = terms_c[chunk, lines].astype(jnp.bfloat16)
        if (step, chunk) in MERGED:
            for b, d in enumerate((1, 3)):
                send(send_c.at[step, chunk, rows(turn(q, 2) * PAIR + b * BLOCK, BLOCK)], passing.at[chunk, b],
                     device(step, p, turn(q, d), z, core), STEP_GROUPS[step], "via", step, chunk)
            for b, d in enumerate((1, 3)):
                send_cubic(step, p, q, chunk, 1 - b, d)
        elif step == 0:
            for d in FAR_FIRST:
                send(send_c.at[0, chunk, rows(turn(q, d) * PAIR, PAIR)], got_c.at[d - 1, chunk],
                     device(0, p, turn(q, d), z, core), STEP_GROUPS[0], "c", 0, chunk)
        else:
            for d in FAR_FIRST:
                for to in (core, other):
                    send(send_c.at[1, chunk, rows(turn(q, d) * PAIR + to * BLOCK, BLOCK)], got_f.at[d - 1, chunk, core],
                         device(1, p, turn(q, d), z, to), STEP_GROUPS[1], "c", 1, chunk)
            send(terms_c.at[chunk, rows(q * PAIR + other * BLOCK, BLOCK)], got_own.at[chunk], device(1, p, q, z, other),
                 STEP_GROUPS[1], "own", chunk)

    def send_cubic(step, p, q, chunk, b, d):
        send(send_c.at[step, chunk, rows(turn(q, d) * PAIR + b * BLOCK, BLOCK)],
             got_c.at[d - 1, chunk, pl.ds(b * BLOCK, BLOCK)],
             device(step, p, turn(q, d), z, core), STEP_GROUPS[step], "c", step, chunk)

    def merge_terms(step, p, q, chunk):
        if (step, chunk) not in MERGED:
            return
        await_copy(passing.at[chunk], "via", step, chunk)
        for b, d in enumerate((1, 3)):
            half = rows(turn(q, d) * PAIR + b * BLOCK, BLOCK)
            send_c[step, chunk, half, :] = (terms_c[chunk, half, :] + passing[chunk, b].astype(jnp.float32)).astype(jnp.bfloat16)
            send_cubic(step, p, q, chunk, b, d)

    def add_cubic(p, q, chunk):
        sources = (1, 3) if (0, chunk) in MERGED else FAR_FIRST
        await_copy(got_c.at[pl.ds(0, len(sources)), chunk], "c", 0, chunk)
        terms = terms_c[chunk, rows(q * PAIR, PAIR), :]
        for d in sources:
            terms += got_c[d - 1, chunk].astype(jnp.float32)
        cols = pl.ds(chunk * BLOCK, BLOCK)
        updated = 1.5 * turned[0, :, cols].astype(jnp.float32) - 0.5 * terms
        for b in range(2):
            part = updated[b * BLOCK:(b + 1) * BLOCK] * keep(block_of(q, z, b), block_of(p, chunk, core))
            unit[1, pl.ds(b * BLOCK, BLOCK), cols] = part.astype(jnp.bfloat16)
        tile_j(q, chunk, core)[...] = unit[1, :, cols]
        send_chunk(chunk, q, p)
        send_unit(1, q, p, cols)

    def share_turned(p, q):
        send(turned.at[1, rows(other * BLOCK, BLOCK)], turned_rest, device(1, p, q, z, other), STEP_GROUPS[1], "turned rest")

    def put_out(p, q, chunk):
        if chunk == 0:
            await_copy(turned_rest, "turned rest")
        await_copy(total(6 * bytes_of(got_own.at[0]) // 2), "c", 1, chunk)
        await_copy(got_own.at[chunk], "own", chunk)
        cols = pl.ds(chunk * BLOCK, BLOCK)
        mine = rows(core * BLOCK, BLOCK)
        for by, terms, state in ((core, terms_c[chunk, rows(q * PAIR + core * BLOCK, BLOCK), :], turned[1, mine, cols]),
                                 (other, got_own[chunk], turned_rest[:, cols])):
            for d in FAR_FIRST:
                terms += got_f[d - 1, chunk, by].astype(jnp.float32)
            updated = 1.5 * state.astype(jnp.float32) - 0.5 * terms
            out[:, rows((2 * chunk + by) * BLOCK, BLOCK)] = updated * keep(block_of(q, z, core), block_of(p, chunk, by))

    for step in range(STEPS):
        p, q = (x, y) if step == 0 else (y, x)
        at = (step, p, q)
        if step == 0:
            gather_first(p, q)
        else:
            finish_chunk(0, p, q)
            pass_chunk_on(2, p, q)
            finish_chunk(1, p, q)
            pass_chunk_on(3, p, q)
            finish_chunk(2, p, q)
            finish_chunk(3, p, q)
            for chunk in range(4):
                await_chunk(chunk, p, q)
            pass_units_on(*at)
        square_terms(*at)
        for strip in range(5):
            add_square(*at, strip)
            if strip == 0 and step == 0:
                pass_units_on(*at)
        cubic_terms(*at, 0)
        add_square(*at, 5)
        add_square(*at, 6)
        cubic_terms(*at, 1)
        if step == 0:
            merge_terms(*at, 0)
            add_square(*at, 7)
            cubic_terms(*at, 2)
            merge_terms(*at, 1)
            await_turned(*at)
            add_cubic(p, q, 0)
            cubic_terms(*at, 3)
            merge_terms(*at, 2)
            add_cubic(p, q, 1)
            merge_terms(*at, 3)
            pass_chunk_on(0, q, p)
            add_cubic(p, q, 2)
            pass_chunk_on(1, q, p)
            add_cubic(p, q, 3)
        else:
            add_square(*at, 7)
            await_turned(*at)
            share_turned(p, q)
            cubic_terms(*at, 2)
            put_out(p, q, 0)
            cubic_terms(*at, 3)
            for chunk in (1, 2, 3):
                put_out(p, q, chunk)

    for group, size in groups.items():
        copy_at(total(size), total(size), GROUPS.index(group), 0, (grid_pos, y)).wait_send()
    assert len(slots) == ARRIVALS, len(slots)
    for step in range(STEPS):
        p, q = (x, y) if step == 0 else (y, x)
        drain_units(step, p, q)


def per_device(density, pattern):
    bf16, f32 = jnp.bfloat16, jnp.float32
    quarter = ORDER // RING
    return pl.pallas_call(
        kernel,
        out_shape=pltpu.VMEM(density.shape, f32),
        in_specs=[pl.BlockSpec(memory_space=pl.ANY)] * 2,
        out_specs=pl.BlockSpec(memory_space=pltpu.VMEM),
        scratch_shapes=[
            pltpu.VMEM(density.shape, bf16),
            pltpu.SMEM(pattern.shape, jnp.int32),
            pltpu.VMEM((STEPS, 4 * BLOCK, quarter), bf16),
            pltpu.VMEM((STEPS, 8 * BLOCK, quarter), bf16),
            pltpu.VMEM((STEPS, 4 * BLOCK, quarter), bf16),
            pltpu.VMEM((STEPS, 3, 4 * BLOCK, PAIR), bf16),
            pltpu.VMEM((4 * BLOCK, quarter), f32),
            pltpu.VMEM((STEPS, 4 * BLOCK, quarter), bf16),
            pltpu.VMEM((STEPS, 4, quarter, BLOCK), bf16),
            pltpu.VMEM((3, 4, PAIR, BLOCK), bf16),
            pltpu.VMEM((4, quarter, BLOCK), f32),
            pltpu.VMEM((4, 2, BLOCK, BLOCK), bf16),
            pltpu.VMEM((3, 4, 2, BLOCK, BLOCK), bf16),
            pltpu.VMEM((4, BLOCK, BLOCK), f32),
            pltpu.VMEM((BLOCK, 4 * BLOCK), bf16),
            pltpu.VMEM((STEPS, PAIR, 4 * BLOCK), bf16),
            pltpu.VMEM((STEPS, 3, PAIR, 4 * BLOCK), bf16),
            pltpu.VMEM((STEPS, PAIR, 4 * BLOCK), bf16),
            pltpu.SemaphoreType.DMA((2,)),
            pltpu.SemaphoreType.DMA((len(GROUPS),)),
            pltpu.SemaphoreType.DMA((ARRIVALS,)),
        ],
        compiler_params=pltpu.CompilerParams(
            collective_id=0, has_side_effects=True, vmem_limit_bytes=56 * 2**20
        ),
        name="polar_steps",
    )(density, pattern)


def solution(mesh):
    placed = (P("grid", "rep"), P())
    return jax.shard_map(
        per_device, mesh=mesh, in_specs=placed, out_specs=P("grid", "rep"), check_vma=False
    )
```

```python
import math

import jax
import jax.numpy as jnp
from jax import lax
from jax.experimental import pallas as pl
from jax.experimental.pallas import tpu as pltpu
from jax.sharding import PartitionSpec as P

BLOCK = 128
STEPS = 2
ORDER = 4096
MESH = pl.DeviceIdType.MESH
RING = 4
PAIR = 2 * BLOCK
HALF = BLOCK // 2
FAR_FIRST = (2, 1, 3)
NEAR_FIRST = (1, 3, 2)

GROUPS = ("first", "second", "step 1", "step 2", "relay", "relay again")
STEP_GROUPS = GROUPS[2:4]
PACED = (0,)
MERGED = ((0,2),(0,3))
ARRIVALS = 67 + len(MERGED)
DIRECT = (2, 3)


def nt_dot(left, right):
    return lax.dot_general(left, right, (((1,), (1,)), ((), ())), preferred_element_type=jnp.float32)


def block_of(outer, z, core):
    return outer * 8 + z * 2 + core


def kernel(density, pattern_in, out, loaded, pattern, rows_i, rows_j, send_q, got_q, terms_q, square, send_c, got_c, terms_c, passing, got_f, got_own, turned_rest,
           unit, relay, turned, halfway, load_sem, send_sem, recv_sem, pace):
    grid_pos = lax.axis_index("grid")
    y = lax.axis_index("rep")
    x = grid_pos // 8
    z = (grid_pos // 2) % 4
    core = grid_pos % 2
    other = 1 - core

    def device(step, p, q, z_at, core_at):
        x_at, y_at = (p, q) if step == 0 else (q, p)
        return ((x_at * 4 + z_at) * 2 + core_at, y_at)

    slots = {}
    groups = {}

    def slot(*key):
        return slots.setdefault(key, len(slots))

    def copy_at(src, dst, group, at, target):
        return pltpu.make_async_remote_copy(
            src_ref=src, dst_ref=dst, send_sem=send_sem.at[group], recv_sem=recv_sem.at[at],
            device_id=target, device_id_type=MESH,
        )

    def rows(start, size):
        return pl.ds(pl.multiple_of(start, size), size)

    def turn(a, d):
        return (a + d) % RING

    barrier = pltpu.get_barrier_semaphore()
    partners = [device(0, x, y, z, other)]
    for d in (1, 2, 3):
        partners += [device(0, turn(x, d), y, z, core), device(0, turn(x, d), y, z, other), device(0, x, turn(y, d), z, core),
                     device(0, x, y, turn(z, d), core), device(0, x, y, turn(z, d), other)]
    for partner in partners:
        pl.semaphore_signal(barrier, inc=1, device_id=partner, device_id_type=MESH)
    loads = [pltpu.make_async_copy(density, loaded, load_sem.at[0]), pltpu.make_async_copy(pattern_in, pattern, load_sem.at[1])]
    for load in loads:
        load.start()
    for load in loads:
        load.wait()

    def keep(row_block, col_block):
        return pattern[row_block, col_block].astype(jnp.float32)

    mine = rows(x * PAIR + core * BLOCK, BLOCK)
    for b in range(8):
        cols = pl.ds(b * BLOCK, BLOCK)
        masked = loaded[:, cols].astype(jnp.float32) * keep(block_of(x, z, core), y * 8 + b)
        rows_j[0, mine, cols] = masked.astype(jnp.bfloat16)
    pl.semaphore_wait(barrier, len(partners))

    def total(size):
        return rows_j.at[:, pl.ds(0, size // (2 * STEPS * rows_j.shape[2]))]

    def bytes_of(ref):
        return math.prod(ref.shape) * jnp.dtype(ref.dtype).itemsize

    def send(src, dst, target, group, *key):
        copy_at(src, dst, GROUPS.index(group), slot(*key), target).start()
        groups[group] = groups.get(group, 0) + bytes_of(src)

    def await_copy(dst, *key):
        copy_at(dst, dst, 0, slot(*key), (grid_pos, y)).wait_recv()

    def gather_first(p, q):
        sibling = device(0, p, q, z, other)

        def target(ring, d):
            return device(0, turn(p, d), q, z, core) if ring == "j" else device(0, p, q, turn(z, d), core)

        def place(ring, d, half, core_at=core):
            if ring == "j":
                return rows_j.at[0, rows(turn(p, d) * PAIR + core_at * BLOCK + half * HALF, HALF)]
            return rows_i.at[0, rows(turn(z, d) * BLOCK + half * HALF, HALF)]

        own = [rows_j.at[0, rows(p * PAIR + core * BLOCK + half * HALF, HALF)] for half in range(2)]
        for d, half in ((1, 0), (3, 1)):
            send(own[half], place("j", 0, half), target("j", d), "first", "near", "j", d)
            send(own[half], place("i", 0, half), target("i", d), "first", "near", "i", d)
        whole = rows_j.at[0, rows(p * PAIR + core * BLOCK, BLOCK)]
        send(whole, whole, sibling, "first", "pair")
        for d, half in ((1, 1), (3, 0)):
            send(own[half], place("j", 0, half), target("j", d), "first", "late", "j")
            send(own[half], place("i", 0, half), target("i", d), "first", "late", "i")
        rows_i[0, rows(z * BLOCK, BLOCK), :] = rows_j[0, rows(p * PAIR + core * BLOCK, BLOCK), :]
        await_copy(rows_j.at[0, rows(p * PAIR + other * BLOCK, BLOCK)], "pair")
        for b in range(4):
            unit[0, :, pl.ds(b * BLOCK, BLOCK)] = rows_j[0, rows(p * PAIR, PAIR), rows((2 * b + core) * BLOCK, BLOCK)]
        send_unit(0, p, q, pl.ds(0, 4 * BLOCK))
        for d, half in ((1, 0), (3, 1)):
            for ring in ("j", "i"):
                here = place(ring, RING - d, half)
                await_copy(here, "near", ring, d)
                send(here, here, target(ring, d), "first", *(("far", "j") if ring == "j" else ("late", "i")))
                if ring == "j":
                    send(here, here, sibling, "first", "shared")
        await_copy(total(2 * bytes_of(own[0])), "late", "j")
        for d, half in ((1, 1), (3, 0)):
            here = place("j", RING - d, half)
            send(here, here, sibling, "first", "shared")
        pass_half_on(p, q)
        await_copy(total(2 * bytes_of(own[0])), "far", "j")
        for half in range(2):
            here = place("j", 2, half)
            send(here, here, sibling, "first", "shared")
        await_copy(total(4 * bytes_of(own[0])), "late", "i")

    def await_shared():
        await_copy(total(6 * HALF * 2 * rows_j.shape[2]), "shared")

    def send_unit(step, p, q, cols):
        lag = turn(p - q, RING)
        at, group = slot("relay", step), GROUPS.index("relay") + step

        @pl.when((lag == 1) | (lag == 3) if step == 0 else lag != 0)
        def _():
            copy_at(unit.at[step, :, cols], relay.at[step, lag - 1, :, cols], group, at, device(step, p, p, z, core)).start()

        if step == 0:
            @pl.when(lag == 2)
            def _():
                for b, d in enumerate((1, 3)):
                    copy_at(unit.at[0, pl.ds(b * BLOCK, BLOCK)], halfway, group, slot("halfway"),
                            device(0, p, turn(q, d), z, core)).start()

    def pass_half_on(p, q):
        lag = turn(p - q, RING)

        @pl.when((lag == 1) | (lag == 3))
        def _():
            await_copy(halfway, "halfway")
            copy_at(halfway, relay.at[0, 1, rows((lag // 2) * BLOCK, BLOCK)], GROUPS.index("relay"), slot("relay", 0),
                    device(0, p, p, z, core)).start()

    def pass_units_on(step, p, q):
        at, onward = slot("relay", step), slot("turned", step)

        @pl.when(p == q)
        def _():
            await_copy(relay.at[step], "relay", step)
            for d in (1, 2, 3):
                copy_at(relay.at[step, d - 1], turned.at[step], GROUPS.index("relay") + step, onward,
                        device(step, turn(p, RING - d), q, z, core)).start()
            turned[step] = unit[step]

    def await_turned(step, p, q):
        slot("turned", step)

        @pl.when(p != q)
        def _():
            await_copy(turned.at[step], "turned", step)

    def drain_units(step, p, q):
        def drain(ref):
            copy_at(ref, ref, GROUPS.index("relay") + step, 0, (grid_pos, y)).wait_send()

        if step == 0:
            lag = turn(p - q, RING)
            pl.when(lag == 2)(lambda: drain(unit.at[0]))
            pl.when((lag == 1) | (lag == 3))(lambda: drain(total(bytes_of(unit.at[0]) + bytes_of(halfway))))
        else:
            pl.when(p != q)(lambda: drain(unit.at[step]))
        pl.when(p == q)(lambda: drain(relay.at[step]))

    def tile_j(p_at, chunk, core_at):
        return rows_j.at[1, rows(p_at * PAIR, PAIR), rows((2 * chunk + core_at) * BLOCK, BLOCK)]

    def tile_i(z_at, chunk, core_at):
        return rows_i.at[1, rows(z_at * BLOCK, BLOCK), rows((2 * chunk + core_at) * BLOCK, BLOCK)]

    def send_chunk(chunk, p, q):
        own = tile_j(p, chunk, core)
        if chunk in DIRECT:
            send(own, own, device(1, turn(p, 2), q, z, core), "second", "far", chunk)
        for d in (1, 3):
            send(own, own, device(1, turn(p, d), q, z, core), "second", "near", chunk)
        send(own, own, device(1, p, q, z, other), "second", "shared again", chunk)
        for d in NEAR_FIRST:
            for to in (core, other):
                src = rows_j.at[1, rows(p * PAIR + to * BLOCK, BLOCK), rows((2 * chunk + core) * BLOCK, BLOCK)]
                send(src, tile_i(z, chunk, core), device(1, p, q, turn(z, d), to), "second", "slab again", chunk)
        tile_i(z, chunk, core)[...] = rows_j[1, rows(p * PAIR + core * BLOCK, BLOCK), rows((2 * chunk + core) * BLOCK, BLOCK)]

    def pass_chunk_on(chunk, p, q):
        await_copy(total(2 * bytes_of(tile_j(p, chunk, core))), "near", chunk)
        for d in (1, 3):
            here = tile_j(turn(p, RING - d), chunk, core)
            if chunk not in DIRECT and (chunk % 2 == 0) == (d == 1):
                send(here, here, device(1, turn(p, d), q, z, core), "second", "far", chunk)
            send(here, here, device(1, p, q, z, other), "second", "shared again", chunk)

    def finish_chunk(chunk, p, q):
        here = tile_j(turn(p, 2), chunk, core)
        await_copy(here, "far", chunk)
        send(here, here, device(1, p, q, z, other), "second", "shared again", chunk)

    def await_chunk(chunk, p, q):
        await_copy(total(4 * bytes_of(tile_j(p, 0, other))), "shared again", chunk)
        tile_i(z, chunk, other)[...] = rows_j[1, rows(p * PAIR + core * BLOCK, BLOCK), rows((2 * chunk + other) * BLOCK, BLOCK)]
        await_copy(total(6 * bytes_of(tile_i(z, 0, core))), "slab again", chunk)

    def square_terms(step, p, q):
        def send_strips(half, first=0, count=PAIR):
            for strip in range(4 * half, 4 * half + 4):
                part = pl.ds(strip * HALF, HALF)
                for d in FAR_FIRST:
                    send(send_q.at[step, part, rows(turn(q, d) * PAIR + first, count)],
                         got_q.at[step, d - 1, part, rows(first, count)],
                         device(step, p, turn(q, d), z, core), STEP_GROUPS[step], "q", step, strip)

        for half in range(2):
            lines = pl.ds(half * PAIR, PAIR)
            if (step, half) == (0, 0):
                for by in (core, other):
                    right = jnp.concatenate([rows_j[0, rows(t * PAIR + by * BLOCK, BLOCK), :] for t in range(RING)], axis=0)
                    value = nt_dot(rows_i[0, lines, :], right)
                    for t in range(RING):
                        cols = rows(t * PAIR + by * BLOCK, BLOCK)
                        piece = value[:, t * BLOCK:(t + 1) * BLOCK]
                        terms_q[lines, cols] = piece
                        send_q[0, lines, cols] = piece.astype(jnp.bfloat16)
                    send_strips(0, by * BLOCK, BLOCK)
                    if by is core:
                        await_shared()
                continue
            terms_q[lines, :] = nt_dot(rows_i[step, lines, :], rows_j[step])
            send_q[step, lines, :] = terms_q[lines, :].astype(jnp.bfloat16)
            send_strips(half)

    def add_square(step, p, q, strip):
        part = pl.ds(strip * HALF, HALF)
        await_copy(got_q.at[step, :, part], "q", step, strip)
        terms = terms_q[part, rows(q * PAIR, PAIR)]
        for d in FAR_FIRST:
            terms += got_q[step, d - 1, part, :].astype(jnp.float32)
        for b in range(2):
            scale = keep(block_of(p, strip // 2, core), block_of(q, z, b)) * (1.0 / ORDER)
            square[step, part, rows(z * PAIR + b * BLOCK, BLOCK)] = (
                terms[:, b * BLOCK:(b + 1) * BLOCK] * scale).astype(jnp.bfloat16)
        if step in PACED and strip % 2 == 1:
            pl.semaphore_signal(pace.at[step], inc=1, device_id=device(step, p, q, z, other), device_id_type=MESH)
        block = square.at[step, part, rows(z * PAIR, PAIR)]
        for d in NEAR_FIRST:
            send(block, block, device(step, p, q, turn(z, d), core), STEP_GROUPS[step], "r", step, strip // 2)

    def cubic_terms(step, p, q, chunk):
        part = pl.ds(chunk * BLOCK, BLOCK)
        if step in PACED:
            pl.semaphore_wait(pace.at[step], 1)
        await_copy(got_q.at[step, :, part], "r", step, chunk)
        for b in range(4):
            lines = pl.ds(b * PAIR, PAIR)
            terms_c[chunk, lines] = nt_dot(rows_j[step, lines, :], square[step, part, :])
            send_c[step, chunk, lines] = terms_c[chunk, lines].astype(jnp.bfloat16)
        if (step, chunk) in MERGED:
            for b, d in enumerate((1, 3)):
                send(send_c.at[step, chunk, rows(turn(q, 2) * PAIR + b * BLOCK, BLOCK)], passing.at[chunk, b],
                     device(step, p, turn(q, d), z, core), STEP_GROUPS[step], "via", step, chunk)
            for b, d in enumerate((1, 3)):
                send_cubic(step, p, q, chunk, 1 - b, d)
        elif step == 0:
            for d in FAR_FIRST:
                send(send_c.at[0, chunk, rows(turn(q, d) * PAIR, PAIR)], got_c.at[d - 1, chunk],
                     device(0, p, turn(q, d), z, core), STEP_GROUPS[0], "c", 0, chunk)
        else:
            for d in FAR_FIRST:
                for to in (core, other):
                    send(send_c.at[1, chunk, rows(turn(q, d) * PAIR + to * BLOCK, BLOCK)], got_f.at[d - 1, chunk, core],
                         device(1, p, turn(q, d), z, to), STEP_GROUPS[1], "c", 1, chunk)
            send(terms_c.at[chunk, rows(q * PAIR + other * BLOCK, BLOCK)], got_own.at[chunk], device(1, p, q, z, other),
                 STEP_GROUPS[1], "own", chunk)

    def send_cubic(step, p, q, chunk, b, d):
        send(send_c.at[step, chunk, rows(turn(q, d) * PAIR + b * BLOCK, BLOCK)],
             got_c.at[d - 1, chunk, pl.ds(b * BLOCK, BLOCK)],
             device(step, p, turn(q, d), z, core), STEP_GROUPS[step], "c", step, chunk)

    def merge_terms(step, p, q, chunk):
        if (step, chunk) not in MERGED:
            return
        await_copy(passing.at[chunk], "via", step, chunk)
        for b, d in enumerate((1, 3)):
            half = rows(turn(q, d) * PAIR + b * BLOCK, BLOCK)
            send_c[step, chunk, half, :] = (terms_c[chunk, half, :] + passing[chunk, b].astype(jnp.float32)).astype(jnp.bfloat16)
            send_cubic(step, p, q, chunk, b, d)

    def add_cubic(p, q, chunk):
        sources = (1, 3) if (0, chunk) in MERGED else FAR_FIRST
        await_copy(got_c.at[pl.ds(0, len(sources)), chunk], "c", 0, chunk)
        terms = terms_c[chunk, rows(q * PAIR, PAIR), :]
        for d in sources:
            terms += got_c[d - 1, chunk].astype(jnp.float32)
        cols = pl.ds(chunk * BLOCK, BLOCK)
        updated = 1.5 * turned[0, :, cols].astype(jnp.float32) - 0.5 * terms
        for b in range(2):
            part = updated[b * BLOCK:(b + 1) * BLOCK] * keep(block_of(q, z, b), block_of(p, chunk, core))
            unit[1, pl.ds(b * BLOCK, BLOCK), cols] = part.astype(jnp.bfloat16)
        tile_j(q, chunk, core)[...] = unit[1, :, cols]
        send_chunk(chunk, q, p)
        send_unit(1, q, p, cols)

    def share_turned(p, q):
        send(turned.at[1, rows(other * BLOCK, BLOCK)], turned_rest, device(1, p, q, z, other), STEP_GROUPS[1], "turned rest")

    def put_out(p, q, chunk):
        if chunk == 0:
            await_copy(turned_rest, "turned rest")
        await_copy(total(6 * bytes_of(got_own.at[0]) // 2), "c", 1, chunk)
        await_copy(got_own.at[chunk], "own", chunk)
        cols = pl.ds(chunk * BLOCK, BLOCK)
        mine = rows(core * BLOCK, BLOCK)
        for by, terms, state in ((core, terms_c[chunk, rows(q * PAIR + core * BLOCK, BLOCK), :], turned[1, mine, cols]),
                                 (other, got_own[chunk], turned_rest[:, cols])):
            for d in FAR_FIRST:
                terms += got_f[d - 1, chunk, by].astype(jnp.float32)
            updated = 1.5 * state.astype(jnp.float32) - 0.5 * terms
            out[:, rows((2 * chunk + by) * BLOCK, BLOCK)] = updated * keep(block_of(q, z, core), block_of(p, chunk, by))

    for step in range(STEPS):
        p, q = (x, y) if step == 0 else (y, x)
        at = (step, p, q)
        if step == 0:
            gather_first(p, q)
        else:
            finish_chunk(0, p, q)
            pass_chunk_on(2, p, q)
            finish_chunk(1, p, q)
            pass_chunk_on(3, p, q)
            finish_chunk(2, p, q)
            finish_chunk(3, p, q)
            for chunk in range(4):
                await_chunk(chunk, p, q)
            pass_units_on(*at)
        square_terms(*at)
        for strip in range(5):
            add_square(*at, strip)
            if strip == 0 and step == 0:
                pass_units_on(*at)
        cubic_terms(*at, 0)
        add_square(*at, 5)
        add_square(*at, 6)
        cubic_terms(*at, 1)
        if step == 0:
            merge_terms(*at, 0)
            add_square(*at, 7)
            cubic_terms(*at, 2)
            merge_terms(*at, 1)
            await_turned(*at)
            add_cubic(p, q, 0)
            cubic_terms(*at, 3)
            merge_terms(*at, 2)
            add_cubic(p, q, 1)
            merge_terms(*at, 3)
            pass_chunk_on(0, q, p)
            add_cubic(p, q, 2)
            pass_chunk_on(1, q, p)
            add_cubic(p, q, 3)
        else:
            add_square(*at, 7)
            await_turned(*at)
            share_turned(p, q)
            cubic_terms(*at, 2)
            put_out(p, q, 0)
            cubic_terms(*at, 3)
            for chunk in (1, 2, 3):
                put_out(p, q, chunk)

    for group, size in groups.items():
        copy_at(total(size), total(size), GROUPS.index(group), 0, (grid_pos, y)).wait_send()
    assert len(slots) == ARRIVALS, len(slots)
    for step in range(STEPS):
        p, q = (x, y) if step == 0 else (y, x)
        drain_units(step, p, q)


def per_device(density, pattern):
    bf16, f32 = jnp.bfloat16, jnp.float32
    quarter = ORDER // RING
    return pl.pallas_call(
        kernel,
        out_shape=pltpu.VMEM(density.shape, f32),
        in_specs=[pl.BlockSpec(memory_space=pl.ANY)] * 2,
        out_specs=pl.BlockSpec(memory_space=pltpu.VMEM),
        scratch_shapes=[
            pltpu.VMEM(density.shape, bf16),
            pltpu.SMEM(pattern.shape, jnp.int32),
            pltpu.VMEM((STEPS, 4 * BLOCK, quarter), bf16),
            pltpu.VMEM((STEPS, 8 * BLOCK, quarter), bf16),
            pltpu.VMEM((STEPS, 4 * BLOCK, quarter), bf16),
            pltpu.VMEM((STEPS, 3, 4 * BLOCK, PAIR), bf16),
            pltpu.VMEM((4 * BLOCK, quarter), f32),
            pltpu.VMEM((STEPS, 4 * BLOCK, quarter), bf16),
            pltpu.VMEM((STEPS, 4, quarter, BLOCK), bf16),
            pltpu.VMEM((3, 4, PAIR, BLOCK), bf16),
            pltpu.VMEM((4, quarter, BLOCK), f32),
            pltpu.VMEM((4, 2, BLOCK, BLOCK), bf16),
            pltpu.VMEM((3, 4, 2, BLOCK, BLOCK), bf16),
            pltpu.VMEM((4, BLOCK, BLOCK), f32),
            pltpu.VMEM((BLOCK, 4 * BLOCK), bf16),
            pltpu.VMEM((STEPS, PAIR, 4 * BLOCK), bf16),
            pltpu.VMEM((STEPS, 3, PAIR, 4 * BLOCK), bf16),
            pltpu.VMEM((STEPS, PAIR, 4 * BLOCK), bf16),
            pltpu.VMEM((BLOCK, 4 * BLOCK), bf16),
            pltpu.SemaphoreType.DMA((2,)),
            pltpu.SemaphoreType.DMA((len(GROUPS),)),
            pltpu.SemaphoreType.DMA((ARRIVALS,)),
            pltpu.SemaphoreType.REGULAR((STEPS,)),
        ],
        compiler_params=pltpu.CompilerParams(
            collective_id=0, has_side_effects=True, vmem_limit_bytes=56 * 2**20
        ),
        name="polar_steps",
    )(density, pattern)


def solution(mesh):
    placed = (P("grid", "rep"), P())
    return jax.shard_map(
        per_device, mesh=mesh, in_specs=placed, out_specs=P("grid", "rep"), check_vma=False
    )
```

```python
import math

import jax
import jax.numpy as jnp
from jax import lax
from jax.experimental import pallas as pl
from jax.experimental.pallas import tpu as pltpu
from jax.sharding import PartitionSpec as P

BLOCK = 128
STEPS = 2
ORDER = 4096
MESH = pl.DeviceIdType.MESH
RING = 4
PAIR = 2 * BLOCK
HALF = BLOCK // 2
FAR_FIRST = (2, 1, 3)
NEAR_FIRST = (2, 1, 3)

GROUPS = ("first", "second", "step 1", "step 2", "relay", "relay again")
STEP_GROUPS = GROUPS[2:4]
PACED = (0,)
MERGED = ((0,2),(0,3))
ARRIVALS = 67 + len(MERGED)
DIRECT = (2, 3)


def nt_dot(left, right):
    return lax.dot_general(left, right, (((1,), (1,)), ((), ())), preferred_element_type=jnp.float32)


def block_of(outer, z, core):
    return outer * 8 + z * 2 + core


def kernel(density, pattern_in, out, loaded, pattern, rows_i, rows_j, send_q, got_q, terms_q, square, send_c, got_c, terms_c, passing, got_f, got_own, turned_rest,
           unit, relay, turned, halfway, load_sem, send_sem, recv_sem, pace):
    grid_pos = lax.axis_index("grid")
    y = lax.axis_index("rep")
    x = grid_pos // 8
    z = (grid_pos // 2) % 4
    core = grid_pos % 2
    other = 1 - core

    def device(step, p, q, z_at, core_at):
        x_at, y_at = (p, q) if step == 0 else (q, p)
        return ((x_at * 4 + z_at) * 2 + core_at, y_at)

    slots = {}
    groups = {}

    def slot(*key):
        return slots.setdefault(key, len(slots))

    def copy_at(src, dst, group, at, target):
        return pltpu.make_async_remote_copy(
            src_ref=src, dst_ref=dst, send_sem=send_sem.at[group], recv_sem=recv_sem.at[at],
            device_id=target, device_id_type=MESH,
        )

    def rows(start, size):
        return pl.ds(pl.multiple_of(start, size), size)

    def turn(a, d):
        return (a + d) % RING

    barrier = pltpu.get_barrier_semaphore()
    partners = [device(0, x, y, z, other)]
    for d in (1, 2, 3):
        partners += [device(0, turn(x, d), y, z, core), device(0, turn(x, d), y, z, other), device(0, x, turn(y, d), z, core),
                     device(0, x, y, turn(z, d), core), device(0, x, y, turn(z, d), other)]
    for partner in partners:
        pl.semaphore_signal(barrier, inc=1, device_id=partner, device_id_type=MESH)
    loads = [pltpu.make_async_copy(density, loaded, load_sem.at[0]), pltpu.make_async_copy(pattern_in, pattern, load_sem.at[1])]
    for load in loads:
        load.start()
    for load in loads:
        load.wait()

    def keep(row_block, col_block):
        return pattern[row_block, col_block].astype(jnp.float32)

    mine = rows(x * PAIR + core * BLOCK, BLOCK)
    for b in range(8):
        cols = pl.ds(b * BLOCK, BLOCK)
        masked = loaded[:, cols].astype(jnp.float32) * keep(block_of(x, z, core), y * 8 + b)
        rows_j[0, mine, cols] = masked.astype(jnp.bfloat16)
    pl.semaphore_wait(barrier, len(partners))

    def total(size):
        return rows_j.at[:, pl.ds(0, size // (2 * STEPS * rows_j.shape[2]))]

    def bytes_of(ref):
        return math.prod(ref.shape) * jnp.dtype(ref.dtype).itemsize

    def send(src, dst, target, group, *key):
        copy_at(src, dst, GROUPS.index(group), slot(*key), target).start()
        groups[group] = groups.get(group, 0) + bytes_of(src)

    def await_copy(dst, *key):
        copy_at(dst, dst, 0, slot(*key), (grid_pos, y)).wait_recv()

    def gather_first(p, q):
        sibling = device(0, p, q, z, other)

        def target(ring, d):
            return device(0, turn(p, d), q, z, core) if ring == "j" else device(0, p, q, turn(z, d), core)

        def place(ring, d, half, core_at=core):
            if ring == "j":
                return rows_j.at[0, rows(turn(p, d) * PAIR + core_at * BLOCK + half * HALF, HALF)]
            return rows_i.at[0, rows(turn(z, d) * BLOCK + half * HALF, HALF)]

        own = [rows_j.at[0, rows(p * PAIR + core * BLOCK + half * HALF, HALF)] for half in range(2)]
        for d, half in ((1, 0), (3, 1)):
            send(own[half], place("j", 0, half), target("j", d), "first", "near", "j", d)
            send(own[half], place("i", 0, half), target("i", d), "first", "near", "i", d)
        whole = rows_j.at[0, rows(p * PAIR + core * BLOCK, BLOCK)]
        send(whole, whole, sibling, "first", "pair")
        for d, half in ((1, 1), (3, 0)):
            send(own[half], place("j", 0, half), target("j", d), "first", "late", "j")
            send(own[half], place("i", 0, half), target("i", d), "first", "late", "i")
        rows_i[0, rows(z * BLOCK, BLOCK), :] = rows_j[0, rows(p * PAIR + core * BLOCK, BLOCK), :]
        await_copy(rows_j.at[0, rows(p * PAIR + other * BLOCK, BLOCK)], "pair")
        for b in range(4):
            unit[0, :, pl.ds(b * BLOCK, BLOCK)] = rows_j[0, rows(p * PAIR, PAIR), rows((2 * b + core) * BLOCK, BLOCK)]
        send_unit(0, p, q, pl.ds(0, 4 * BLOCK))
        for d, half in ((1, 0), (3, 1)):
            for ring in ("j", "i"):
                here = place(ring, RING - d, half)
                await_copy(here, "near", ring, d)
                send(here, here, target(ring, d), "first", *(("far", "j") if ring == "j" else ("late", "i")))
                if ring == "j":
                    send(here, here, sibling, "first", "shared")
        await_copy(total(2 * bytes_of(own[0])), "late", "j")
        for d, half in ((1, 1), (3, 0)):
            here = place("j", RING - d, half)
            send(here, here, sibling, "first", "shared")
        pass_half_on(p, q)
        await_copy(total(2 * bytes_of(own[0])), "far", "j")
        for half in range(2):
            here = place("j", 2, half)
            send(here, here, sibling, "first", "shared")
        await_copy(total(4 * bytes_of(own[0])), "late", "i")

    def await_shared():
        await_copy(total(6 * HALF * 2 * rows_j.shape[2]), "shared")

    def send_unit(step, p, q, cols):
        lag = turn(p - q, RING)
        at, group = slot("relay", step), GROUPS.index("relay") + step

        @pl.when((lag == 1) | (lag == 3) if step == 0 else lag != 0)
        def _():
            copy_at(unit.at[step, :, cols], relay.at[step, lag - 1, :, cols], group, at, device(step, p, p, z, core)).start()

        if step == 0:
            @pl.when(lag == 2)
            def _():
                for b, d in enumerate((1, 3)):
                    copy_at(unit.at[0, pl.ds(b * BLOCK, BLOCK)], halfway, group, slot("halfway"),
                            device(0, p, turn(q, d), z, core)).start()

    def pass_half_on(p, q):
        lag = turn(p - q, RING)

        @pl.when((lag == 1) | (lag == 3))
        def _():
            await_copy(halfway, "halfway")
            copy_at(halfway, relay.at[0, 1, rows((lag // 2) * BLOCK, BLOCK)], GROUPS.index("relay"), slot("relay", 0),
                    device(0, p, p, z, core)).start()

    def pass_units_on(step, p, q):
        at, onward = slot("relay", step), slot("turned", step)

        @pl.when(p == q)
        def _():
            await_copy(relay.at[step], "relay", step)
            for d in (1, 2, 3):
                copy_at(relay.at[step, d - 1], turned.at[step], GROUPS.index("relay") + step, onward,
                        device(step, turn(p, RING - d), q, z, core)).start()
            turned[step] = unit[step]

    def await_turned(step, p, q):
        slot("turned", step)

        @pl.when(p != q)
        def _():
            await_copy(turned.at[step], "turned", step)

    def drain_units(step, p, q):
        def drain(ref):
            copy_at(ref, ref, GROUPS.index("relay") + step, 0, (grid_pos, y)).wait_send()

        if step == 0:
            lag = turn(p - q, RING)
            pl.when(lag == 2)(lambda: drain(unit.at[0]))
            pl.when((lag == 1) | (lag == 3))(lambda: drain(total(bytes_of(unit.at[0]) + bytes_of(halfway))))
        else:
            pl.when(p != q)(lambda: drain(unit.at[step]))
        pl.when(p == q)(lambda: drain(relay.at[step]))

    def tile_j(p_at, chunk, core_at):
        return rows_j.at[1, rows(p_at * PAIR, PAIR), rows((2 * chunk + core_at) * BLOCK, BLOCK)]

    def tile_i(z_at, chunk, core_at):
        return rows_i.at[1, rows(z_at * BLOCK, BLOCK), rows((2 * chunk + core_at) * BLOCK, BLOCK)]

    def send_chunk(chunk, p, q):
        own = tile_j(p, chunk, core)
        if chunk in DIRECT:
            send(own, own, device(1, turn(p, 2), q, z, core), "second", "far", chunk)
        for d in (1, 3):
            send(own, own, device(1, turn(p, d), q, z, core), "second", "near", chunk)
        send(own, own, device(1, p, q, z, other), "second", "shared again", chunk)
        for d in NEAR_FIRST:
            for to in (core, other):
                src = rows_j.at[1, rows(p * PAIR + to * BLOCK, BLOCK), rows((2 * chunk + core) * BLOCK, BLOCK)]
                send(src, tile_i(z, chunk, core), device(1, p, q, turn(z, d), to), "second", "slab again", chunk)
        tile_i(z, chunk, core)[...] = rows_j[1, rows(p * PAIR + core * BLOCK, BLOCK), rows((2 * chunk + core) * BLOCK, BLOCK)]

    def pass_chunk_on(chunk, p, q):
        await_copy(total(2 * bytes_of(tile_j(p, chunk, core))), "near", chunk)
        for d in (1, 3):
            here = tile_j(turn(p, RING - d), chunk, core)
            if chunk not in DIRECT and (chunk % 2 == 0) == (d == 1):
                send(here, here, device(1, turn(p, d), q, z, core), "second", "far", chunk)
            send(here, here, device(1, p, q, z, other), "second", "shared again", chunk)

    def finish_chunk(chunk, p, q):
        here = tile_j(turn(p, 2), chunk, core)
        await_copy(here, "far", chunk)
        send(here, here, device(1, p, q, z, other), "second", "shared again", chunk)

    def await_chunk(chunk, p, q):
        await_copy(total(4 * bytes_of(tile_j(p, 0, other))), "shared again", chunk)
        tile_i(z, chunk, other)[...] = rows_j[1, rows(p * PAIR + core * BLOCK, BLOCK), rows((2 * chunk + other) * BLOCK, BLOCK)]
        await_copy(total(6 * bytes_of(tile_i(z, 0, core))), "slab again", chunk)

    def square_terms(step, p, q):
        def send_strips(half, first=0, count=PAIR):
            for strip in range(4 * half, 4 * half + 4):
                part = pl.ds(strip * HALF, HALF)
                for d in FAR_FIRST:
                    send(send_q.at[step, part, rows(turn(q, d) * PAIR + first, count)],
                         got_q.at[step, d - 1, part, rows(first, count)],
                         device(step, p, turn(q, d), z, core), STEP_GROUPS[step], "q", step, strip)

        for half in range(2):
            lines = pl.ds(half * PAIR, PAIR)
            if (step, half) == (0, 0):
                for by in (core, other):
                    right = jnp.concatenate([rows_j[0, rows(t * PAIR + by * BLOCK, BLOCK), :] for t in range(RING)], axis=0)
                    value = nt_dot(rows_i[0, lines, :], right)
                    for t in range(RING):
                        cols = rows(t * PAIR + by * BLOCK, BLOCK)
                        piece = value[:, t * BLOCK:(t + 1) * BLOCK]
                        terms_q[lines, cols] = piece
                        send_q[0, lines, cols] = piece.astype(jnp.bfloat16)
                    send_strips(0, by * BLOCK, BLOCK)
                    if by is core:
                        await_shared()
                continue
            terms_q[lines, :] = nt_dot(rows_i[step, lines, :], rows_j[step])
            send_q[step, lines, :] = terms_q[lines, :].astype(jnp.bfloat16)
            send_strips(half)

    def add_square(step, p, q, strip):
        part = pl.ds(strip * HALF, HALF)
        await_copy(got_q.at[step, :, part], "q", step, strip)
        terms = terms_q[part, rows(q * PAIR, PAIR)]
        for d in FAR_FIRST:
            terms += got_q[step, d - 1, part, :].astype(jnp.float32)
        for b in range(2):
            scale = keep(block_of(p, strip // 2, core), block_of(q, z, b)) * (1.0 / ORDER)
            square[step, part, rows(z * PAIR + b * BLOCK, BLOCK)] = (
                terms[:, b * BLOCK:(b + 1) * BLOCK] * scale).astype(jnp.bfloat16)
        if step in PACED and strip % 2 == 1:
            pl.semaphore_signal(pace.at[step], inc=1, device_id=device(step, p, q, z, other), device_id_type=MESH)
        block = square.at[step, part, rows(z * PAIR, PAIR)]
        for d in NEAR_FIRST:
            send(block, block, device(step, p, q, turn(z, d), core), STEP_GROUPS[step], "r", step, strip // 2)

    def cubic_terms(step, p, q, chunk):
        part = pl.ds(chunk * BLOCK, BLOCK)
        if step in PACED:
            pl.semaphore_wait(pace.at[step], 1)
        await_copy(got_q.at[step, :, part], "r", step, chunk)
        for b in range(4):
            lines = pl.ds(b * PAIR, PAIR)
            terms_c[chunk, lines] = nt_dot(rows_j[step, lines, :], square[step, part, :])
            send_c[step, chunk, lines] = terms_c[chunk, lines].astype(jnp.bfloat16)
        if (step, chunk) in MERGED:
            for b, d in enumerate((1, 3)):
                send(send_c.at[step, chunk, rows(turn(q, 2) * PAIR + b * BLOCK, BLOCK)], passing.at[chunk, b],
                     device(step, p, turn(q, d), z, core), STEP_GROUPS[step], "via", step, chunk)
            for b, d in enumerate((1, 3)):
                send_cubic(step, p, q, chunk, 1 - b, d)
        elif step == 0:
            for d in FAR_FIRST:
                send(send_c.at[0, chunk, rows(turn(q, d) * PAIR, PAIR)], got_c.at[d - 1, chunk],
                     device(0, p, turn(q, d), z, core), STEP_GROUPS[0], "c", 0, chunk)
        else:
            for d in FAR_FIRST:
                for to in (core, other):
                    send(send_c.at[1, chunk, rows(turn(q, d) * PAIR + to * BLOCK, BLOCK)], got_f.at[d - 1, chunk, core],
                         device(1, p, turn(q, d), z, to), STEP_GROUPS[1], "c", 1, chunk)
            send(terms_c.at[chunk, rows(q * PAIR + other * BLOCK, BLOCK)], got_own.at[chunk], device(1, p, q, z, other),
                 STEP_GROUPS[1], "own", chunk)

    def send_cubic(step, p, q, chunk, b, d):
        send(send_c.at[step, chunk, rows(turn(q, d) * PAIR + b * BLOCK, BLOCK)],
             got_c.at[d - 1, chunk, pl.ds(b * BLOCK, BLOCK)],
             device(step, p, turn(q, d), z, core), STEP_GROUPS[step], "c", step, chunk)

    def merge_terms(step, p, q, chunk):
        if (step, chunk) not in MERGED:
            return
        await_copy(passing.at[chunk], "via", step, chunk)
        for b, d in enumerate((1, 3)):
            half = rows(turn(q, d) * PAIR + b * BLOCK, BLOCK)
            send_c[step, chunk, half, :] = (terms_c[chunk, half, :] + passing[chunk, b].astype(jnp.float32)).astype(jnp.bfloat16)
            send_cubic(step, p, q, chunk, b, d)

    def add_cubic(p, q, chunk):
        sources = (1, 3) if (0, chunk) in MERGED else FAR_FIRST
        await_copy(got_c.at[pl.ds(0, len(sources)), chunk], "c", 0, chunk)
        terms = terms_c[chunk, rows(q * PAIR, PAIR), :]
        for d in sources:
            terms += got_c[d - 1, chunk].astype(jnp.float32)
        cols = pl.ds(chunk * BLOCK, BLOCK)
        updated = 1.5 * turned[0, :, cols].astype(jnp.float32) - 0.5 * terms
        for b in range(2):
            part = updated[b * BLOCK:(b + 1) * BLOCK] * keep(block_of(q, z, b), block_of(p, chunk, core))
            unit[1, pl.ds(b * BLOCK, BLOCK), cols] = part.astype(jnp.bfloat16)
        tile_j(q, chunk, core)[...] = unit[1, :, cols]
        send_chunk(chunk, q, p)
        send_unit(1, q, p, cols)

    def share_turned(p, q):
        send(turned.at[1, rows(other * BLOCK, BLOCK)], turned_rest, device(1, p, q, z, other), STEP_GROUPS[1], "turned rest")

    def put_out(p, q, chunk):
        if chunk == 0:
            await_copy(turned_rest, "turned rest")
        await_copy(total(6 * bytes_of(got_own.at[0]) // 2), "c", 1, chunk)
        await_copy(got_own.at[chunk], "own", chunk)
        cols = pl.ds(chunk * BLOCK, BLOCK)
        mine = rows(core * BLOCK, BLOCK)
        for by, terms, state in ((core, terms_c[chunk, rows(q * PAIR + core * BLOCK, BLOCK), :], turned[1, mine, cols]),
                                 (other, got_own[chunk], turned_rest[:, cols])):
            for d in FAR_FIRST:
                terms += got_f[d - 1, chunk, by].astype(jnp.float32)
            updated = 1.5 * state.astype(jnp.float32) - 0.5 * terms
            out[:, rows((2 * chunk + by) * BLOCK, BLOCK)] = updated * keep(block_of(q, z, core), block_of(p, chunk, by))

    for step in range(STEPS):
        p, q = (x, y) if step == 0 else (y, x)
        at = (step, p, q)
        if step == 0:
            gather_first(p, q)
        else:
            finish_chunk(0, p, q)
            pass_chunk_on(2, p, q)
            finish_chunk(1, p, q)
            pass_chunk_on(3, p, q)
            finish_chunk(2, p, q)
            finish_chunk(3, p, q)
            for chunk in range(4):
                await_chunk(chunk, p, q)
            pass_units_on(*at)
        square_terms(*at)
        for strip in range(5):
            add_square(*at, strip)
            if strip == 0 and step == 0:
                pass_units_on(*at)
        cubic_terms(*at, 0)
        add_square(*at, 5)
        add_square(*at, 6)
        cubic_terms(*at, 1)
        if step == 0:
            merge_terms(*at, 0)
            add_square(*at, 7)
            cubic_terms(*at, 2)
            merge_terms(*at, 1)
            await_turned(*at)
            add_cubic(p, q, 0)
            cubic_terms(*at, 3)
            merge_terms(*at, 2)
            add_cubic(p, q, 1)
            merge_terms(*at, 3)
            pass_chunk_on(0, q, p)
            add_cubic(p, q, 2)
            pass_chunk_on(1, q, p)
            add_cubic(p, q, 3)
        else:
            add_square(*at, 7)
            await_turned(*at)
            share_turned(p, q)
            cubic_terms(*at, 2)
            put_out(p, q, 0)
            cubic_terms(*at, 3)
            for chunk in (1, 2, 3):
                put_out(p, q, chunk)

    for group, size in groups.items():
        copy_at(total(size), total(size), GROUPS.index(group), 0, (grid_pos, y)).wait_send()
    assert len(slots) == ARRIVALS, len(slots)
    for step in range(STEPS):
        p, q = (x, y) if step == 0 else (y, x)
        drain_units(step, p, q)


def per_device(density, pattern):
    bf16, f32 = jnp.bfloat16, jnp.float32
    quarter = ORDER // RING
    return pl.pallas_call(
        kernel,
        out_shape=pltpu.VMEM(density.shape, f32),
        in_specs=[pl.BlockSpec(memory_space=pl.ANY)] * 2,
        out_specs=pl.BlockSpec(memory_space=pltpu.VMEM),
        scratch_shapes=[
            pltpu.VMEM(density.shape, bf16),
            pltpu.SMEM(pattern.shape, jnp.int32),
            pltpu.VMEM((STEPS, 4 * BLOCK, quarter), bf16),
            pltpu.VMEM((STEPS, 8 * BLOCK, quarter), bf16),
            pltpu.VMEM((STEPS, 4 * BLOCK, quarter), bf16),
            pltpu.VMEM((STEPS, 3, 4 * BLOCK, PAIR), bf16),
            pltpu.VMEM((4 * BLOCK, quarter), f32),
            pltpu.VMEM((STEPS, 4 * BLOCK, quarter), bf16),
            pltpu.VMEM((STEPS, 4, quarter, BLOCK), bf16),
            pltpu.VMEM((3, 4, PAIR, BLOCK), bf16),
            pltpu.VMEM((4, quarter, BLOCK), f32),
            pltpu.VMEM((4, 2, BLOCK, BLOCK), bf16),
            pltpu.VMEM((3, 4, 2, BLOCK, BLOCK), bf16),
            pltpu.VMEM((4, BLOCK, BLOCK), f32),
            pltpu.VMEM((BLOCK, 4 * BLOCK), bf16),
            pltpu.VMEM((STEPS, PAIR, 4 * BLOCK), bf16),
            pltpu.VMEM((STEPS, 3, PAIR, 4 * BLOCK), bf16),
            pltpu.VMEM((STEPS, PAIR, 4 * BLOCK), bf16),
            pltpu.VMEM((BLOCK, 4 * BLOCK), bf16),
            pltpu.SemaphoreType.DMA((2,)),
            pltpu.SemaphoreType.DMA((len(GROUPS),)),
            pltpu.SemaphoreType.DMA((ARRIVALS,)),
            pltpu.SemaphoreType.REGULAR((STEPS,)),
        ],
        compiler_params=pltpu.CompilerParams(
            collective_id=0, has_side_effects=True, vmem_limit_bytes=56 * 2**20
        ),
        name="polar_steps",
    )(density, pattern)


def solution(mesh):
    placed = (P("grid", "rep"), P())
    return jax.shard_map(
        per_device, mesh=mesh, in_specs=placed, out_specs=P("grid", "rep"), check_vma=False
    )
```

```python
import math

import jax
import jax.numpy as jnp
from jax import lax
from jax.experimental import pallas as pl
from jax.experimental.pallas import tpu as pltpu
from jax.sharding import PartitionSpec as P

BLOCK = 128
STEPS = 2
ORDER = 4096
MESH = pl.DeviceIdType.MESH
RING = 4
PAIR = 2 * BLOCK
HALF = BLOCK // 2
FAR_FIRST = (2, 1, 3)
NEAR_FIRST = (2, 1, 3)

GROUPS = ("first", "second", "step 1", "step 2", "relay", "relay again")
STEP_GROUPS = GROUPS[2:4]
PACED = (0,)
ARRIVALS = 67
DIRECT = (2, 3)


def nt_dot(left, right):
    return lax.dot_general(left, right, (((1,), (1,)), ((), ())), preferred_element_type=jnp.float32)


def block_of(outer, z, core):
    return outer * 8 + z * 2 + core


def kernel(density, pattern_in, out, loaded, pattern, rows_i, rows_j, got_q, terms_q, square, got_c, terms_c, got_f, got_own, turned_rest,
           unit, relay, turned, halfway, load_sem, send_sem, recv_sem, pace):
    grid_pos = lax.axis_index("grid")
    y = lax.axis_index("rep")
    x = grid_pos // 8
    z = (grid_pos // 2) % 4
    core = grid_pos % 2
    other = 1 - core

    def device(step, p, q, z_at, core_at):
        x_at, y_at = (p, q) if step == 0 else (q, p)
        return ((x_at * 4 + z_at) * 2 + core_at, y_at)

    slots = {}
    groups = {}

    def slot(*key):
        return slots.setdefault(key, len(slots))

    def copy_at(src, dst, group, at, target):
        return pltpu.make_async_remote_copy(
            src_ref=src, dst_ref=dst, send_sem=send_sem.at[group], recv_sem=recv_sem.at[at],
            device_id=target, device_id_type=MESH,
        )

    def rows(start, size):
        return pl.ds(pl.multiple_of(start, size), size)

    def turn(a, d):
        return (a + d) % RING

    barrier = pltpu.get_barrier_semaphore()
    partners = [device(0, x, y, z, other)]
    for d in (1, 2, 3):
        partners += [device(0, turn(x, d), y, z, core), device(0, turn(x, d), y, z, other), device(0, x, turn(y, d), z, core),
                     device(0, x, y, turn(z, d), core), device(0, x, y, turn(z, d), other)]
    for partner in partners:
        pl.semaphore_signal(barrier, inc=1, device_id=partner, device_id_type=MESH)
    loads = [pltpu.make_async_copy(density, loaded, load_sem.at[0]), pltpu.make_async_copy(pattern_in, pattern, load_sem.at[1])]
    for load in loads:
        load.start()
    for load in loads:
        load.wait()

    def keep(row_block, col_block):
        return pattern[row_block, col_block].astype(jnp.float32)

    mine = rows(x * PAIR + core * BLOCK, BLOCK)
    for b in range(8):
        cols = pl.ds(b * BLOCK, BLOCK)
        masked = loaded[:, cols].astype(jnp.float32) * keep(block_of(x, z, core), y * 8 + b)
        rows_j[0, mine, cols] = masked.astype(jnp.bfloat16)
    pl.semaphore_wait(barrier, len(partners))

    def total(size):
        return rows_j.at[:, pl.ds(0, size // (2 * STEPS * rows_j.shape[2]))]

    def bytes_of(ref):
        return math.prod(ref.shape) * jnp.dtype(ref.dtype).itemsize

    def send(src, dst, target, group, *key):
        copy_at(src, dst, GROUPS.index(group), slot(*key), target).start()
        groups[group] = groups.get(group, 0) + bytes_of(src)

    def await_copy(dst, *key):
        copy_at(dst, dst, 0, slot(*key), (grid_pos, y)).wait_recv()

    def gather_first(p, q):
        sibling = device(0, p, q, z, other)

        def target(ring, d):
            return device(0, turn(p, d), q, z, core) if ring == "j" else device(0, p, q, turn(z, d), core)

        def place(ring, d, half, core_at=core):
            if ring == "j":
                return rows_j.at[0, rows(turn(p, d) * PAIR + core_at * BLOCK + half * HALF, HALF)]
            return rows_i.at[0, rows(turn(z, d) * BLOCK + half * HALF, HALF)]

        own = [rows_j.at[0, rows(p * PAIR + core * BLOCK + half * HALF, HALF)] for half in range(2)]
        for d, half in ((1, 0), (3, 1)):
            send(own[half], place("j", 0, half), target("j", d), "first", "near", "j", d)
            send(own[half], place("i", 0, half), target("i", d), "first", "near", "i", d)
        whole = rows_j.at[0, rows(p * PAIR + core * BLOCK, BLOCK)]
        send(whole, whole, sibling, "first", "pair")
        for d, half in ((1, 1), (3, 0)):
            send(own[half], place("j", 0, half), target("j", d), "first", "late", "j")
            send(own[half], place("i", 0, half), target("i", d), "first", "late", "i")
        rows_i[0, rows(z * BLOCK, BLOCK), :] = rows_j[0, rows(p * PAIR + core * BLOCK, BLOCK), :]
        await_copy(rows_j.at[0, rows(p * PAIR + other * BLOCK, BLOCK)], "pair")
        for b in range(4):
            unit[0, :, pl.ds(b * BLOCK, BLOCK)] = rows_j[0, rows(p * PAIR, PAIR), rows((2 * b + core) * BLOCK, BLOCK)]
        send_unit(0, p, q, pl.ds(0, 4 * BLOCK))
        for d, half in ((1, 0), (3, 1)):
            for ring in ("j", "i"):
                here = place(ring, RING - d, half)
                await_copy(here, "near", ring, d)
                send(here, here, target(ring, d), "first", *(("far", "j") if ring == "j" else ("late", "i")))
                if ring == "j":
                    send(here, here, sibling, "first", "shared")
        await_copy(total(2 * bytes_of(own[0])), "late", "j")
        for d, half in ((1, 1), (3, 0)):
            here = place("j", RING - d, half)
            send(here, here, sibling, "first", "shared")
        pass_half_on(p, q)
        await_copy(total(2 * bytes_of(own[0])), "far", "j")
        for half in range(2):
            here = place("j", 2, half)
            send(here, here, sibling, "first", "shared")
        await_copy(total(4 * bytes_of(own[0])), "late", "i")

    def await_shared():
        await_copy(total(6 * HALF * 2 * rows_j.shape[2]), "shared")

    def send_unit(step, p, q, cols):
        lag = turn(p - q, RING)
        at, group = slot("relay", step), GROUPS.index("relay") + step

        @pl.when((lag == 1) | (lag == 3) if step == 0 else lag != 0)
        def _():
            copy_at(unit.at[step, :, cols], relay.at[step, lag - 1, :, cols], group, at, device(step, p, p, z, core)).start()

        if step == 0:
            @pl.when(lag == 2)
            def _():
                for b, d in enumerate((1, 3)):
                    copy_at(unit.at[0, pl.ds(b * BLOCK, BLOCK)], halfway, group, slot("halfway"),
                            device(0, p, turn(q, d), z, core)).start()

    def pass_half_on(p, q):
        lag = turn(p - q, RING)

        @pl.when((lag == 1) | (lag == 3))
        def _():
            await_copy(halfway, "halfway")
            copy_at(halfway, relay.at[0, 1, rows((lag // 2) * BLOCK, BLOCK)], GROUPS.index("relay"), slot("relay", 0),
                    device(0, p, p, z, core)).start()

    def pass_units_on(step, p, q):
        at, onward = slot("relay", step), slot("turned", step)

        @pl.when(p == q)
        def _():
            await_copy(relay.at[step], "relay", step)
            for d in (1, 2, 3):
                copy_at(relay.at[step, d - 1], turned.at[step], GROUPS.index("relay") + step, onward,
                        device(step, turn(p, RING - d), q, z, core)).start()
            turned[step] = unit[step]

    def await_turned(step, p, q):
        slot("turned", step)

        @pl.when(p != q)
        def _():
            await_copy(turned.at[step], "turned", step)

    def drain_units(step, p, q):
        def drain(ref):
            copy_at(ref, ref, GROUPS.index("relay") + step, 0, (grid_pos, y)).wait_send()

        if step == 0:
            lag = turn(p - q, RING)
            pl.when(lag == 2)(lambda: drain(unit.at[0]))
            pl.when((lag == 1) | (lag == 3))(lambda: drain(total(bytes_of(unit.at[0]) + bytes_of(halfway))))
        else:
            pl.when(p != q)(lambda: drain(unit.at[step]))
        pl.when(p == q)(lambda: drain(relay.at[step]))

    def tile_j(p_at, chunk, core_at):
        return rows_j.at[1, rows(p_at * PAIR, PAIR), rows((2 * chunk + core_at) * BLOCK, BLOCK)]

    def tile_i(z_at, chunk, core_at):
        return rows_i.at[1, rows(z_at * BLOCK, BLOCK), rows((2 * chunk + core_at) * BLOCK, BLOCK)]

    def send_chunk(chunk, p, q):
        own = tile_j(p, chunk, core)
        if chunk in DIRECT:
            send(own, own, device(1, turn(p, 2), q, z, core), "second", "far", chunk)
        for d in (1, 3):
            send(own, own, device(1, turn(p, d), q, z, core), "second", "near", chunk)
        send(own, own, device(1, p, q, z, other), "second", "shared again", chunk)
        for d in NEAR_FIRST:
            for to in (core, other):
                src = rows_j.at[1, rows(p * PAIR + to * BLOCK, BLOCK), rows((2 * chunk + core) * BLOCK, BLOCK)]
                send(src, tile_i(z, chunk, core), device(1, p, q, turn(z, d), to), "second", "slab again", chunk)
        tile_i(z, chunk, core)[...] = rows_j[1, rows(p * PAIR + core * BLOCK, BLOCK), rows((2 * chunk + core) * BLOCK, BLOCK)]

    def pass_chunk_on(chunk, p, q):
        await_copy(total(2 * bytes_of(tile_j(p, chunk, core))), "near", chunk)
        for d in (1, 3):
            here = tile_j(turn(p, RING - d), chunk, core)
            if chunk not in DIRECT and (chunk % 2 == 0) == (d == 1):
                send(here, here, device(1, turn(p, d), q, z, core), "second", "far", chunk)
            send(here, here, device(1, p, q, z, other), "second", "shared again", chunk)

    def finish_chunk(chunk, p, q):
        here = tile_j(turn(p, 2), chunk, core)
        await_copy(here, "far", chunk)
        send(here, here, device(1, p, q, z, other), "second", "shared again", chunk)

    def await_chunk(chunk, p, q):
        await_copy(total(4 * bytes_of(tile_j(p, 0, other))), "shared again", chunk)
        tile_i(z, chunk, other)[...] = rows_j[1, rows(p * PAIR + core * BLOCK, BLOCK), rows((2 * chunk + other) * BLOCK, BLOCK)]
        await_copy(total(6 * bytes_of(tile_i(z, 0, core))), "slab again", chunk)

    def square_terms(step, p, q):
        def send_strips(half, first=0, count=PAIR):
            for strip in range(4 * half, 4 * half + 4):
                part = pl.ds(strip * HALF, HALF)
                for d in FAR_FIRST:
                    send(terms_q.at[step, part, rows(turn(q, d) * PAIR + first, count)],
                         got_q.at[step, d - 1, part, rows(first, count)],
                         device(step, p, turn(q, d), z, core), STEP_GROUPS[step], "q", step, strip)

        for half in range(2):
            lines = pl.ds(half * PAIR, PAIR)
            if (step, half) == (0, 0):
                for by in (core, other):
                    right = jnp.concatenate([rows_j[0, rows(t * PAIR + by * BLOCK, BLOCK), :] for t in range(RING)], axis=0)
                    value = nt_dot(rows_i[0, lines, :], right)
                    for t in range(RING):
                        cols = rows(t * PAIR + by * BLOCK, BLOCK)
                        piece = value[:, t * BLOCK:(t + 1) * BLOCK]
                        terms_q[step, lines, cols] = piece
                    send_strips(0, by * BLOCK, BLOCK)
                    if by is core:
                        await_shared()
                continue
            terms_q[step, lines, :] = nt_dot(rows_i[step, lines, :], rows_j[step])
            send_strips(half)

    def add_square(step, p, q, strip):
        part = pl.ds(strip * HALF, HALF)
        await_copy(got_q.at[step, :, part], "q", step, strip)
        terms = terms_q[step, part, rows(q * PAIR, PAIR)]
        for d in FAR_FIRST:
            terms += got_q[step, d - 1, part, :]
        for b in range(2):
            scale = keep(block_of(p, strip // 2, core), block_of(q, z, b)) * (1.0 / ORDER)
            square[step, part, rows(z * PAIR + b * BLOCK, BLOCK)] = (
                terms[:, b * BLOCK:(b + 1) * BLOCK] * scale).astype(jnp.bfloat16)
        if step in PACED and strip % 2 == 1:
            pl.semaphore_signal(pace.at[step], inc=1, device_id=device(step, p, q, z, other), device_id_type=MESH)
        block = square.at[step, part, rows(z * PAIR, PAIR)]
        for d in NEAR_FIRST:
            send(block, block, device(step, p, q, turn(z, d), core), ("step 1", "first")[step], "r", step, strip // 2)

    def cubic_terms(step, p, q, chunk):
        part = pl.ds(chunk * BLOCK, BLOCK)
        if step in PACED:
            pl.semaphore_wait(pace.at[step], 1)
        await_copy(total(3 * BLOCK * PAIR * 2), "r", step, chunk)
        for b in range(4):
            lines = pl.ds(b * PAIR, PAIR)
            terms_c[step, chunk, lines] = nt_dot(rows_j[step, lines, :], square[step, part, :])
        if step == 0:
            for d in FAR_FIRST:
                send(terms_c.at[0, chunk, rows(turn(q, d) * PAIR, PAIR)], got_c.at[d - 1, chunk],
                     device(0, p, turn(q, d), z, core), STEP_GROUPS[0], "c", 0, chunk)
        else:
            for d in FAR_FIRST:
                for to in (core, other):
                    send(terms_c.at[1, chunk, rows(turn(q, d) * PAIR + to * BLOCK, BLOCK)], got_f.at[d - 1, chunk, core],
                         device(1, p, turn(q, d), z, to), STEP_GROUPS[1], "c", 1, chunk)
            send(terms_c.at[1, chunk, rows(q * PAIR + other * BLOCK, BLOCK)], got_own.at[chunk], device(1, p, q, z, other),
                 STEP_GROUPS[1], "own", chunk)

    def add_cubic(p, q, chunk):
        sources = FAR_FIRST
        await_copy(got_c.at[pl.ds(0, len(sources)), chunk], "c", 0, chunk)
        terms = terms_c[0, chunk, rows(q * PAIR, PAIR), :]
        for d in sources:
            terms += got_c[d - 1, chunk]
        cols = pl.ds(chunk * BLOCK, BLOCK)
        updated = 1.5 * turned[0, :, cols].astype(jnp.float32) - 0.5 * terms
        for b in range(2):
            part = updated[b * BLOCK:(b + 1) * BLOCK] * keep(block_of(q, z, b), block_of(p, chunk, core))
            unit[1, pl.ds(b * BLOCK, BLOCK), cols] = part.astype(jnp.bfloat16)
        tile_j(q, chunk, core)[...] = unit[1, :, cols]
        send_chunk(chunk, q, p)
        send_unit(1, q, p, cols)

    def share_turned(p, q):
        send(turned.at[1, rows(other * BLOCK, BLOCK)], turned_rest, device(1, p, q, z, other), STEP_GROUPS[1], "turned rest")

    def put_out(p, q, chunk):
        if chunk == 0:
            await_copy(turned_rest, "turned rest")
        await_copy(total(6 * bytes_of(got_own.at[0])), "c", 1, chunk)
        await_copy(got_own.at[chunk], "own", chunk)
        cols = pl.ds(chunk * BLOCK, BLOCK)
        mine = rows(core * BLOCK, BLOCK)
        for by, terms, state in ((core, terms_c[1, chunk, rows(q * PAIR + core * BLOCK, BLOCK), :], turned[1, mine, cols]),
                                 (other, got_own[chunk], turned_rest[:, cols])):
            for d in FAR_FIRST:
                terms += got_f[d - 1, chunk, by]
            updated = 1.5 * state.astype(jnp.float32) - 0.5 * terms
            out[:, rows((2 * chunk + by) * BLOCK, BLOCK)] = updated * keep(block_of(q, z, core), block_of(p, chunk, by))

    for step in range(STEPS):
        p, q = (x, y) if step == 0 else (y, x)
        at = (step, p, q)
        if step == 0:
            gather_first(p, q)
        else:
            finish_chunk(0, p, q)
            pass_chunk_on(2, p, q)
            finish_chunk(1, p, q)
            pass_chunk_on(3, p, q)
            finish_chunk(2, p, q)
            finish_chunk(3, p, q)
            for chunk in range(4):
                await_chunk(chunk, p, q)
            pass_units_on(*at)
        square_terms(*at)
        for strip in range(5):
            add_square(*at, strip)
            if strip == 0 and step == 0:
                pass_units_on(*at)
        cubic_terms(*at, 0)
        add_square(*at, 5)
        add_square(*at, 6)
        cubic_terms(*at, 1)
        if step == 0:
            add_square(*at, 7)
            cubic_terms(*at, 2)
            await_turned(*at)
            add_cubic(p, q, 0)
            cubic_terms(*at, 3)
            add_cubic(p, q, 1)
            pass_chunk_on(0, q, p)
            add_cubic(p, q, 2)
            pass_chunk_on(1, q, p)
            add_cubic(p, q, 3)
        else:
            add_square(*at, 7)
            await_turned(*at)
            share_turned(p, q)
            cubic_terms(*at, 2)
            put_out(p, q, 0)
            cubic_terms(*at, 3)
            for chunk in (1, 2, 3):
                put_out(p, q, chunk)

    for group, size in groups.items():
        copy_at(total(size), total(size), GROUPS.index(group), 0, (grid_pos, y)).wait_send()
    assert len(slots) == ARRIVALS, len(slots)
    for step in range(STEPS):
        p, q = (x, y) if step == 0 else (y, x)
        drain_units(step, p, q)


def per_device(density, pattern):
    bf16, f32 = jnp.bfloat16, jnp.float32
    quarter = ORDER // RING
    return pl.pallas_call(
        kernel,
        out_shape=pltpu.VMEM(density.shape, f32),
        in_specs=[pl.BlockSpec(memory_space=pl.ANY)] * 2,
        out_specs=pl.BlockSpec(memory_space=pltpu.VMEM),
        scratch_shapes=[
            pltpu.VMEM(density.shape, bf16),
            pltpu.SMEM(pattern.shape, jnp.int32),
            pltpu.VMEM((STEPS, 4 * BLOCK, quarter), bf16),
            pltpu.VMEM((STEPS, 8 * BLOCK, quarter), bf16),
            pltpu.VMEM((STEPS, 3, 4 * BLOCK, PAIR), f32),
            pltpu.VMEM((STEPS, 4 * BLOCK, quarter), f32),
            pltpu.VMEM((STEPS, 4 * BLOCK, quarter), bf16),
            pltpu.VMEM((3, 4, PAIR, BLOCK), f32),
            pltpu.VMEM((STEPS, 4, quarter, BLOCK), f32),
            pltpu.VMEM((3, 4, 2, BLOCK, BLOCK), f32),
            pltpu.VMEM((4, BLOCK, BLOCK), f32),
            pltpu.VMEM((BLOCK, 4 * BLOCK), bf16),
            pltpu.VMEM((STEPS, PAIR, 4 * BLOCK), bf16),
            pltpu.VMEM((STEPS, 3, PAIR, 4 * BLOCK), bf16),
            pltpu.VMEM((STEPS, PAIR, 4 * BLOCK), bf16),
            pltpu.VMEM((BLOCK, 4 * BLOCK), bf16),
            pltpu.SemaphoreType.DMA((2,)),
            pltpu.SemaphoreType.DMA((len(GROUPS),)),
            pltpu.SemaphoreType.DMA((ARRIVALS,)),
            pltpu.SemaphoreType.REGULAR((STEPS,)),
        ],
        compiler_params=pltpu.CompilerParams(
            collective_id=0, has_side_effects=True, vmem_limit_bytes=56 * 2**20
        ),
        name="polar_steps",
    )(density, pattern)


def solution(mesh):
    placed = (P("grid", "rep"), P())
    return jax.shard_map(
        per_device, mesh=mesh, in_specs=placed, out_specs=P("grid", "rep"), check_vma=False
    )
```

```python
import math

import jax
import jax.numpy as jnp
from jax import lax
from jax.experimental import pallas as pl
from jax.experimental.pallas import tpu as pltpu
from jax.sharding import PartitionSpec as P

BLOCK = 128
STEPS = 2
ORDER = 4096
MESH = pl.DeviceIdType.MESH
RING = 4
PAIR = 2 * BLOCK
HALF = BLOCK // 2
FAR_FIRST = (2, 1, 3)
NEAR_FIRST = (2, 1, 3)

GROUPS = ("first", "second", "step 1", "step 2", "relay", "relay again")
STEP_GROUPS = GROUPS[2:4]
MERGED = ((0,2),(0,3))
ARRIVALS = 61 + len(MERGED)
DIRECT = (2, 3)


def nt_dot(left, right):
    return lax.dot_general(left, right, (((1,), (1,)), ((), ())), preferred_element_type=jnp.float32)


def block_of(outer, z, core):
    return outer * 8 + z * 2 + core


def kernel(density, pattern_in, out, loaded, pattern, rows_i, rows_j, send_q, got_q, terms_q, square, send_c, got_c, terms_c, passing, got_f, got_own, turned_rest,
           unit, relay, turned, halfway, load_sem, send_sem, recv_sem):
    grid_pos = lax.axis_index("grid")
    y = lax.axis_index("rep")
    x = grid_pos // 8
    z = (grid_pos // 2) % 4
    core = grid_pos % 2
    other = 1 - core

    def device(step, p, q, z_at, core_at):
        x_at, y_at = (p, q) if step == 0 else (q, p)
        return ((x_at * 4 + z_at) * 2 + core_at, y_at)

    slots = {}
    groups = {}

    def slot(*key):
        return slots.setdefault(key, len(slots))

    def copy_at(src, dst, group, at, target):
        return pltpu.make_async_remote_copy(
            src_ref=src, dst_ref=dst, send_sem=send_sem.at[group], recv_sem=recv_sem.at[at],
            device_id=target, device_id_type=MESH,
        )

    def rows(start, size):
        return pl.ds(pl.multiple_of(start, size), size)

    def turn(a, d):
        return (a + d) % RING

    barrier = pltpu.get_barrier_semaphore()
    partners = [device(0, x, y, z, other)]
    for d in (1, 2, 3):
        partners += [device(0, turn(x, d), y, z, core), device(0, turn(x, d), y, z, other), device(0, x, turn(y, d), z, core),
                     device(0, x, y, turn(z, d), core), device(0, x, y, turn(z, d), other)]
    for partner in partners:
        pl.semaphore_signal(barrier, inc=1, device_id=partner, device_id_type=MESH)
    loads = [pltpu.make_async_copy(density, loaded, load_sem.at[0]), pltpu.make_async_copy(pattern_in, pattern, load_sem.at[1])]
    for load in loads:
        load.start()
    for load in loads:
        load.wait()

    def keep(row_block, col_block):
        return pattern[row_block, col_block].astype(jnp.float32)

    mine = rows(x * PAIR + core * BLOCK, BLOCK)
    for b in range(8):
        cols = pl.ds(b * BLOCK, BLOCK)
        masked = loaded[:, cols].astype(jnp.float32) * keep(block_of(x, z, core), y * 8 + b)
        rows_j[0, mine, cols] = masked.astype(jnp.bfloat16)
    pl.semaphore_wait(barrier, len(partners))

    def total(size):
        return rows_j.at[:, pl.ds(0, size // (2 * STEPS * rows_j.shape[2]))]

    def bytes_of(ref):
        return math.prod(ref.shape) * jnp.dtype(ref.dtype).itemsize

    def send(src, dst, target, group, *key):
        copy_at(src, dst, GROUPS.index(group), slot(*key), target).start()
        groups[group] = groups.get(group, 0) + bytes_of(src)

    def await_copy(dst, *key):
        copy_at(dst, dst, 0, slot(*key), (grid_pos, y)).wait_recv()

    def gather_first(p, q):
        sibling = device(0, p, q, z, other)

        def target(ring, d):
            return device(0, turn(p, d), q, z, core) if ring == "j" else device(0, p, q, turn(z, d), core)

        def place(ring, d, half, core_at=core):
            if ring == "j":
                return rows_j.at[0, rows(turn(p, d) * PAIR + core_at * BLOCK + half * HALF, HALF)]
            return rows_i.at[0, rows(turn(z, d) * BLOCK + half * HALF, HALF)]

        own = [rows_j.at[0, rows(p * PAIR + core * BLOCK + half * HALF, HALF)] for half in range(2)]
        for d, half in ((1, 0), (3, 1)):
            send(own[half], place("j", 0, half), target("j", d), "first", "near", "j", d)
            send(own[half], place("i", 0, half), target("i", d), "first", "near", "i", d)
        whole = rows_j.at[0, rows(p * PAIR + core * BLOCK, BLOCK)]
        send(whole, whole, sibling, "first", "pair")
        for d, half in ((1, 1), (3, 0)):
            send(own[half], place("j", 0, half), target("j", d), "first", "late", "j")
            send(own[half], place("i", 0, half), target("i", d), "first", "late", "i")
        rows_i[0, rows(z * BLOCK, BLOCK), :] = rows_j[0, rows(p * PAIR + core * BLOCK, BLOCK), :]
        await_copy(rows_j.at[0, rows(p * PAIR + other * BLOCK, BLOCK)], "pair")
        for b in range(4):
            unit[0, :, pl.ds(b * BLOCK, BLOCK)] = rows_j[0, rows(p * PAIR, PAIR), rows((2 * b + core) * BLOCK, BLOCK)]
        send_unit(0, p, q, pl.ds(0, 4 * BLOCK))
        for d, half in ((1, 0), (3, 1)):
            for ring in ("j", "i"):
                here = place(ring, RING - d, half)
                await_copy(here, "near", ring, d)
                send(here, here, target(ring, d), "first", *(("far", "j") if ring == "j" else ("late", "i")))
                if ring == "j":
                    send(here, here, sibling, "first", "shared")
        await_copy(total(2 * bytes_of(own[0])), "late", "j")
        for d, half in ((1, 1), (3, 0)):
            here = place("j", RING - d, half)
            send(here, here, sibling, "first", "shared")
        pass_half_on(p, q)
        await_copy(total(2 * bytes_of(own[0])), "far", "j")
        for half in range(2):
            here = place("j", 2, half)
            send(here, here, sibling, "first", "shared")
        await_copy(total(4 * bytes_of(own[0])), "late", "i")

    def await_shared():
        await_copy(total(6 * HALF * 2 * rows_j.shape[2]), "shared")

    def send_unit(step, p, q, cols):
        lag = turn(p - q, RING)
        at, group = slot("relay", step), GROUPS.index("relay") + step

        @pl.when((lag == 1) | (lag == 3) if step == 0 else lag != 0)
        def _():
            copy_at(unit.at[step, :, cols], relay.at[step, lag - 1, :, cols], group, at, device(step, p, p, z, core)).start()

        if step == 0:
            @pl.when(lag == 2)
            def _():
                for b, d in enumerate((1, 3)):
                    copy_at(unit.at[0, pl.ds(b * BLOCK, BLOCK)], halfway, group, slot("halfway"),
                            device(0, p, turn(q, d), z, core)).start()

    def pass_half_on(p, q):
        lag = turn(p - q, RING)

        @pl.when((lag == 1) | (lag == 3))
        def _():
            await_copy(halfway, "halfway")
            copy_at(halfway, relay.at[0, 1, rows((lag // 2) * BLOCK, BLOCK)], GROUPS.index("relay"), slot("relay", 0),
                    device(0, p, p, z, core)).start()

    def pass_units_on(step, p, q):
        at, onward = slot("relay", step), slot("turned", step)

        @pl.when(p == q)
        def _():
            await_copy(relay.at[step], "relay", step)
            for d in (1, 2, 3):
                copy_at(relay.at[step, d - 1], turned.at[step], GROUPS.index("relay") + step, onward,
                        device(step, turn(p, RING - d), q, z, core)).start()
            turned[step] = unit[step]

    def await_turned(step, p, q):
        slot("turned", step)

        @pl.when(p != q)
        def _():
            await_copy(turned.at[step], "turned", step)

    def drain_units(step, p, q):
        def drain(ref):
            copy_at(ref, ref, GROUPS.index("relay") + step, 0, (grid_pos, y)).wait_send()

        if step == 0:
            lag = turn(p - q, RING)
            pl.when(lag == 2)(lambda: drain(unit.at[0]))
            pl.when((lag == 1) | (lag == 3))(lambda: drain(total(bytes_of(unit.at[0]) + bytes_of(halfway))))
        else:
            pl.when(p != q)(lambda: drain(unit.at[step]))
        pl.when(p == q)(lambda: drain(relay.at[step]))

    def tile_j(p_at, chunk, core_at):
        return rows_j.at[1, rows(p_at * PAIR, PAIR), rows((2 * chunk + core_at) * BLOCK, BLOCK)]

    def tile_i(z_at, chunk, core_at):
        return rows_i.at[1, rows(z_at * BLOCK, BLOCK), rows((2 * chunk + core_at) * BLOCK, BLOCK)]

    def send_chunk(chunk, p, q):
        own = tile_j(p, chunk, core)
        if chunk in DIRECT:
            send(own, own, device(1, turn(p, 2), q, z, core), "second", "far", chunk)
        for d in (1, 3):
            send(own, own, device(1, turn(p, d), q, z, core), "second", "near", chunk)
        send(own, own, device(1, p, q, z, other), "second", "shared again")
        for d in NEAR_FIRST:
            for to in (core, other):
                src = rows_j.at[1, rows(p * PAIR + to * BLOCK, BLOCK), rows((2 * chunk + core) * BLOCK, BLOCK)]
                send(src, tile_i(z, chunk, core), device(1, p, q, turn(z, d), to), "second", "slab again")
        tile_i(z, chunk, core)[...] = rows_j[1, rows(p * PAIR + core * BLOCK, BLOCK), rows((2 * chunk + core) * BLOCK, BLOCK)]

    def pass_chunk_on(chunk, p, q):
        await_copy(total(2 * bytes_of(tile_j(p, chunk, core))), "near", chunk)
        for d in (1, 3):
            here = tile_j(turn(p, RING - d), chunk, core)
            if chunk not in DIRECT and (chunk % 2 == 0) == (d == 1):
                send(here, here, device(1, turn(p, d), q, z, core), "second", "far", chunk)
            send(here, here, device(1, p, q, z, other), "second", "shared again")

    def finish_chunk(chunk, p, q):
        here = tile_j(turn(p, 2), chunk, core)
        await_copy(here, "far", chunk)
        send(here, here, device(1, p, q, z, other), "second", "shared again")

    def await_chunks(p, q):
        await_copy(total(16 * bytes_of(tile_j(p, 0, other))), "shared again")
        for chunk in range(4):
            tile_i(z, chunk, other)[...] = rows_j[1, rows(p * PAIR + core * BLOCK, BLOCK), rows((2 * chunk + other) * BLOCK, BLOCK)]
        await_copy(total(24 * bytes_of(tile_i(z, 0, core))), "slab again")

    def square_terms(step, p, q):
        def send_strips(half, first=0, count=PAIR):
            for strip in range(4 * half, 4 * half + 4):
                part = pl.ds(strip * HALF, HALF)
                for d in FAR_FIRST:
                    send(send_q.at[step, part, rows(turn(q, d) * PAIR + first, count)],
                         got_q.at[step, d - 1, part, rows(first, count)],
                         device(step, p, turn(q, d), z, core), STEP_GROUPS[step], "q", step, strip)

        for half in range(2):
            lines = pl.ds(half * PAIR, PAIR)
            if (step, half) == (0, 0):
                for by in (core, other):
                    right = jnp.concatenate([rows_j[0, rows(t * PAIR + by * BLOCK, BLOCK), :] for t in range(RING)], axis=0)
                    value = nt_dot(rows_i[0, lines, :], right)
                    for t in range(RING):
                        cols = rows(t * PAIR + by * BLOCK, BLOCK)
                        piece = value[:, t * BLOCK:(t + 1) * BLOCK]
                        terms_q[lines, cols] = piece
                        send_q[0, lines, cols] = piece.astype(jnp.bfloat16)
                    send_strips(0, by * BLOCK, BLOCK)
                    if by is core:
                        await_shared()
                continue
            terms_q[lines, :] = nt_dot(rows_i[step, lines, :], rows_j[step])
            send_q[step, lines, :] = terms_q[lines, :].astype(jnp.bfloat16)
            send_strips(half)

    def add_square(step, p, q, strip):
        part = pl.ds(strip * HALF, HALF)
        await_copy(got_q.at[step, :, part], "q", step, strip)
        terms = terms_q[part, rows(q * PAIR, PAIR)]
        for d in FAR_FIRST:
            terms += got_q[step, d - 1, part, :].astype(jnp.float32)
        for b in range(2):
            scale = keep(block_of(p, strip // 2, core), block_of(q, z, b)) * (1.0 / ORDER)
            square[step, part, rows(z * PAIR + b * BLOCK, BLOCK)] = (
                terms[:, b * BLOCK:(b + 1) * BLOCK] * scale).astype(jnp.bfloat16)
        block = square.at[step, part, rows(z * PAIR, PAIR)]
        for d in NEAR_FIRST:
            send(block, block, device(step, p, q, turn(z, d), core), STEP_GROUPS[step], "r", step, strip // 2)

    def cubic_terms(step, p, q, chunk):
        part = pl.ds(chunk * BLOCK, BLOCK)
        await_copy(got_q.at[step, :, part], "r", step, chunk)
        for b in range(4):
            lines = pl.ds(b * PAIR, PAIR)
            terms_c[chunk, lines] = nt_dot(rows_j[step, lines, :], square[step, part, :])
            send_c[step, chunk, lines] = terms_c[chunk, lines].astype(jnp.bfloat16)
        if (step, chunk) in MERGED:
            for b, d in enumerate((1, 3)):
                send(send_c.at[step, chunk, rows(turn(q, 2) * PAIR + b * BLOCK, BLOCK)], passing.at[chunk, b],
                     device(step, p, turn(q, d), z, core), STEP_GROUPS[step], "via", step, chunk)
            for b, d in enumerate((1, 3)):
                send_cubic(step, p, q, chunk, 1 - b, d)
        elif step == 0:
            for d in FAR_FIRST:
                send(send_c.at[0, chunk, rows(turn(q, d) * PAIR, PAIR)], got_c.at[d - 1, chunk],
                     device(0, p, turn(q, d), z, core), STEP_GROUPS[0], "c", 0, chunk)
        else:
            for d in FAR_FIRST:
                for to in (core, other):
                    send(send_c.at[1, chunk, rows(turn(q, d) * PAIR + to * BLOCK, BLOCK)], got_f.at[d - 1, chunk, core],
                         device(1, p, turn(q, d), z, to), STEP_GROUPS[1], "c", 1, chunk)
            send(terms_c.at[chunk, rows(q * PAIR + other * BLOCK, BLOCK)], got_own.at[chunk], device(1, p, q, z, other),
                 STEP_GROUPS[1], "own", chunk)

    def send_cubic(step, p, q, chunk, b, d):
        send(send_c.at[step, chunk, rows(turn(q, d) * PAIR + b * BLOCK, BLOCK)],
             got_c.at[d - 1, chunk, pl.ds(b * BLOCK, BLOCK)],
             device(step, p, turn(q, d), z, core), STEP_GROUPS[step], "c", step, chunk)

    def merge_terms(step, p, q, chunk):
        if (step, chunk) not in MERGED:
            return
        await_copy(passing.at[chunk], "via", step, chunk)
        for b, d in enumerate((1, 3)):
            half = rows(turn(q, d) * PAIR + b * BLOCK, BLOCK)
            send_c[step, chunk, half, :] = (terms_c[chunk, half, :] + passing[chunk, b].astype(jnp.float32)).astype(jnp.bfloat16)
            send_cubic(step, p, q, chunk, b, d)

    def add_cubic(p, q, chunk):
        sources = (1, 3) if (0, chunk) in MERGED else FAR_FIRST
        await_copy(got_c.at[pl.ds(0, len(sources)), chunk], "c", 0, chunk)
        terms = terms_c[chunk, rows(q * PAIR, PAIR), :]
        for d in sources:
            terms += got_c[d - 1, chunk].astype(jnp.float32)
        cols = pl.ds(chunk * BLOCK, BLOCK)
        updated = 1.5 * turned[0, :, cols].astype(jnp.float32) - 0.5 * terms
        for b in range(2):
            part = updated[b * BLOCK:(b + 1) * BLOCK] * keep(block_of(q, z, b), block_of(p, chunk, core))
            unit[1, pl.ds(b * BLOCK, BLOCK), cols] = part.astype(jnp.bfloat16)
        tile_j(q, chunk, core)[...] = unit[1, :, cols]
        send_chunk(chunk, q, p)
        send_unit(1, q, p, cols)

    def share_turned(p, q):
        send(turned.at[1, rows(other * BLOCK, BLOCK)], turned_rest, device(1, p, q, z, other), STEP_GROUPS[1], "turned rest")

    def put_out(p, q, chunk):
        if chunk == 0:
            await_copy(turned_rest, "turned rest")
        await_copy(total(6 * bytes_of(got_own.at[0]) // 2), "c", 1, chunk)
        await_copy(got_own.at[chunk], "own", chunk)
        cols = pl.ds(chunk * BLOCK, BLOCK)
        mine = rows(core * BLOCK, BLOCK)
        for by, terms, state in ((core, terms_c[chunk, rows(q * PAIR + core * BLOCK, BLOCK), :], turned[1, mine, cols]),
                                 (other, got_own[chunk], turned_rest[:, cols])):
            for d in FAR_FIRST:
                terms += got_f[d - 1, chunk, by].astype(jnp.float32)
            updated = 1.5 * state.astype(jnp.float32) - 0.5 * terms
            out[:, rows((2 * chunk + by) * BLOCK, BLOCK)] = updated * keep(block_of(q, z, core), block_of(p, chunk, by))

    for step in range(STEPS):
        p, q = (x, y) if step == 0 else (y, x)
        at = (step, p, q)
        if step == 0:
            gather_first(p, q)
        else:
            finish_chunk(0, p, q)
            pass_chunk_on(2, p, q)
            finish_chunk(1, p, q)
            pass_chunk_on(3, p, q)
            finish_chunk(2, p, q)
            finish_chunk(3, p, q)
            await_chunks(p, q)
            pass_units_on(*at)
        square_terms(*at)
        for strip in range(5):
            add_square(*at, strip)
            if strip == 0 and step == 0:
                pass_units_on(*at)
        cubic_terms(*at, 0)
        add_square(*at, 5)
        add_square(*at, 6)
        cubic_terms(*at, 1)
        if step == 0:
            merge_terms(*at, 0)
            add_square(*at, 7)
            cubic_terms(*at, 2)
            merge_terms(*at, 1)
            await_turned(*at)
            add_cubic(p, q, 0)
            cubic_terms(*at, 3)
            merge_terms(*at, 2)
            add_cubic(p, q, 1)
            merge_terms(*at, 3)
            pass_chunk_on(0, q, p)
            add_cubic(p, q, 2)
            pass_chunk_on(1, q, p)
            add_cubic(p, q, 3)
        else:
            add_square(*at, 7)
            await_turned(*at)
            share_turned(p, q)
            cubic_terms(*at, 2)
            put_out(p, q, 0)
            cubic_terms(*at, 3)
            for chunk in (1, 2, 3):
                put_out(p, q, chunk)

    for group, size in groups.items():
        copy_at(total(size), total(size), GROUPS.index(group), 0, (grid_pos, y)).wait_send()
    assert len(slots) == ARRIVALS, len(slots)
    for step in range(STEPS):
        p, q = (x, y) if step == 0 else (y, x)
        drain_units(step, p, q)


def per_device(density, pattern):
    bf16, f32 = jnp.bfloat16, jnp.float32
    quarter = ORDER // RING
    return pl.pallas_call(
        kernel,
        out_shape=pltpu.VMEM(density.shape, f32),
        in_specs=[pl.BlockSpec(memory_space=pl.ANY)] * 2,
        out_specs=pl.BlockSpec(memory_space=pltpu.VMEM),
        scratch_shapes=[
            pltpu.VMEM(density.shape, bf16),
            pltpu.SMEM(pattern.shape, jnp.int32),
            pltpu.VMEM((STEPS, 4 * BLOCK, quarter), bf16),
            pltpu.VMEM((STEPS, 8 * BLOCK, quarter), bf16),
            pltpu.VMEM((STEPS, 4 * BLOCK, quarter), bf16),
            pltpu.VMEM((STEPS, 3, 4 * BLOCK, PAIR), bf16),
            pltpu.VMEM((4 * BLOCK, quarter), f32),
            pltpu.VMEM((STEPS, 4 * BLOCK, quarter), bf16),
            pltpu.VMEM((STEPS, 4, quarter, BLOCK), bf16),
            pltpu.VMEM((3, 4, PAIR, BLOCK), bf16),
            pltpu.VMEM((4, quarter, BLOCK), f32),
            pltpu.VMEM((4, 2, BLOCK, BLOCK), bf16),
            pltpu.VMEM((3, 4, 2, BLOCK, BLOCK), bf16),
            pltpu.VMEM((4, BLOCK, BLOCK), f32),
            pltpu.VMEM((BLOCK, 4 * BLOCK), bf16),
            pltpu.VMEM((STEPS, PAIR, 4 * BLOCK), bf16),
            pltpu.VMEM((STEPS, 3, PAIR, 4 * BLOCK), bf16),
            pltpu.VMEM((STEPS, PAIR, 4 * BLOCK), bf16),
            pltpu.VMEM((BLOCK, 4 * BLOCK), bf16),
            pltpu.SemaphoreType.DMA((2,)),
            pltpu.SemaphoreType.DMA((len(GROUPS),)),
            pltpu.SemaphoreType.DMA((ARRIVALS,)),
        ],
        compiler_params=pltpu.CompilerParams(
            collective_id=0, has_side_effects=True, vmem_limit_bytes=56 * 2**20
        ),
        name="polar_steps",
    )(density, pattern)


def solution(mesh):
    placed = (P("grid", "rep"), P())
    return jax.shard_map(
        per_device, mesh=mesh, in_specs=placed, out_specs=P("grid", "rep"), check_vma=False
    )
```
